128 devices in a mesh: dp: 8 (over y, x_lo), tm: 16 (over z, x_hi, core).
Axes of the slice: x: 4 (x_hi: 2, x_lo: 2; x = x_hi * 2 + x_lo), y: 4, z: 4, core: 2. Of those that a mesh axis runs over, the one named last changes fastest.
Arguments:
- queries: bfloat16 [8, 16, 256, 16, 128], P('dp', 'tm'), may hold values from -200 to 200
- keys: bfloat16 [8, 16, 256, 16, 128], P('dp', 'tm'), may hold values from -6.5 to 6.5
- values: bfloat16 [8, 16, 256, 16, 128], P('dp', 'tm'), may hold values from -6 to 6
- out_weight: bfloat16 [2048, 16, 128], replicated, may hold values from -0.125 to 0.125
- grad_out: bfloat16 [8, 16, 256, 2048], P('dp', 'tm'), may hold values from -6 to 6
Outputs:
- grad_queries: bfloat16 [8, 16, 256, 16, 128], P('dp', 'tm')
- grad_keys: bfloat16 [8, 16, 256, 16, 128], P('dp', 'tm')
- grad_values: bfloat16 [8, 16, 256, 16, 128], P('dp', 'tm')
- grad_weight: float32 [2048, 16, 128], P(('dp', 'tm'))
The draws below stay inside these ranges and needn't reach their ends.
All inputs are finite; a program needn't handle non-finite values.
Results may differ from the reference program's by a relative error of at most 0.0058.
Values may be sent and summed in bfloat16 or wider, within the bound.
No kernel may reach another device: no remote copies, remote signals or barrier semaphores. Data moves between devices by JAX's collectives and lax.ppermute only.
A program may use at most 128 MiB of HBM per device.

```python
import jax
import jax.numpy as jnp
from jax import lax

PATCH = 256
HEADS = 16
E = 128
DM = 2048
FRAMES = 16
CLIPS = 8


def shared_keys(key):
    return jax.random.truncated_normal(jax.random.fold_in(key, 11), -6.0, 6.0, (CLIPS, FRAMES, PATCH, HEADS, E), jnp.float32)


def draw_keys(key, part):
    base = shared_keys(key)
    return base.astype(jnp.bfloat16)


def draw_queries(key, part):
    base = shared_keys(key)
    key = jax.random.fold_in(key, 7)
    fresh = jax.random.truncated_normal(key, -6.0, 6.0, base.shape, jnp.float32)
    return fresh.astype(jnp.bfloat16)


def strengthened(entries, key, source, target, blocks, factor):
    owner, partner = [(jnp.arange(entries.shape[axis_at]) // (entries.shape[axis_at] // blocks)).reshape([-1 if axis == axis_at else 1 for axis in range(entries.ndim)]) for axis_at in (source, target)]
    chosen = jax.random.permutation(key, blocks)[partner]
    strong = (owner == chosen) | (owner == (partner + blocks // 2) % blocks)
    return jnp.where(strong, factor * entries, entries)


def block_scale(stream_key, extent, pieces, low, largest):
    factor_of, own = 1.0, jax.random.fold_in(stream_key, 6)
    for dim, shards_of in pieces:
        draws = jnp.exp(jax.random.uniform(jax.random.fold_in(own, dim), (shards_of,), jnp.float32, low / len(pieces), largest / len(pieces)))
        factor_of = factor_of * jnp.repeat(draws, extent[dim] // shards_of).reshape([-1 if axis == dim else 1 for axis in range(len(extent))])
    return factor_of


def scatter_about(key, extent, deviation, most, pieces=(), kind=jnp.bfloat16):
    array = deviation * jax.random.normal(key, extent, jnp.float32)
    if pieces:
        array = array * block_scale(key, extent, pieces, -0.22, 0.18)
    return jnp.clip(array, -most, most).astype(kind)


def noise_with(key, shape, deviation, reach, cuts, heavy, dtype=jnp.bfloat16):
    result = deviation * jax.random.normal(key, shape, jnp.float32)
    if cuts:
        result = result * block_scale(key, shape, cuts, -0.22, 0.18)
    return jnp.clip(strengthened(result, jax.random.fold_in(key, 3), *heavy), -reach, reach).astype(dtype)


def setup_inputs(seed: int = 0) -> dict:
    streams_of = jax.random.split(jax.random.key(seed), 6)
    return {
        "queries": draw_queries(jax.random.fold_in(streams_of[5], 71), 0),
        "keys": draw_keys(jax.random.fold_in(streams_of[5], 71), 0),
        "values": scatter_about(streams_of[2], (CLIPS, FRAMES, PATCH, HEADS, E), 1.0, 6.0, ((0, 8), (1, 16))),
        "out_weight": scatter_about(streams_of[3], (DM, HEADS, E), (HEADS * E) ** -0.5, 0.125),
        "grad_out": noise_with(streams_of[4], (CLIPS, FRAMES, PATCH, DM), 1.0, 6.0, ((0, 8), (1, 16)), (1, 3, 16, 2.0)),
    }


def one_clip(queries, keys, values, out_weight, grad_out):
    scale = 1.0 / jnp.sqrt(jnp.float32(E))
    q32 = queries.astype(jnp.float32)
    k32 = keys.astype(jnp.float32)
    v32 = values.astype(jnp.float32)
    g32 = grad_out.astype(jnp.float32)
    grad_attended = jnp.einsum('fpd,dhe->fphe', g32, out_weight.astype(jnp.float32)).astype(jnp.bfloat16)
    ga32 = grad_attended.astype(jnp.float32)
    scores = jnp.einsum('iphe,jphe->phij', q32, k32) * scale
    frame_ids = jnp.arange(FRAMES)
    causal = frame_ids[None, :] <= frame_ids[:, None]
    masked = jnp.where(causal, scores, -jnp.inf)
    top = lax.optimization_barrier(jnp.max(masked, axis=-1, keepdims=True))
    expd = jnp.where(causal, jnp.exp(masked - top), 0.0)
    probs = expd / lax.optimization_barrier(jnp.sum(expd, axis=-1, keepdims=True))
    weights = probs.astype(jnp.bfloat16).astype(jnp.float32)
    attended = jnp.einsum('phij,jphe->iphe', weights, v32).astype(jnp.bfloat16)
    term = jnp.einsum('fpd,fphe->dhe', g32, attended.astype(jnp.float32))
    grad_values = jnp.einsum('phij,iphe->jphe', weights, ga32).astype(jnp.bfloat16)
    grad_probs = jnp.einsum('iphe,jphe->phij', ga32, v32)
    delta = lax.optimization_barrier(jnp.sum(probs * grad_probs, axis=-1, keepdims=True))
    grad_scores = (probs * (grad_probs - delta)).astype(jnp.bfloat16).astype(jnp.float32)
    grad_queries = (jnp.einsum('phij,jphe->iphe', grad_scores, k32) * scale).astype(jnp.bfloat16)
    grad_keys = (jnp.einsum('phij,iphe->jphe', grad_scores, q32) * scale).astype(jnp.bfloat16)
    return (grad_queries, grad_keys, grad_values, term)

def reference(queries, keys, values, out_weight, grad_out):

    def step(total, inputs):
        grad_q, grad_k, grad_v, term = one_clip(inputs[0], inputs[1], inputs[2], out_weight, inputs[3])
        return (total + term, (grad_q, grad_k, grad_v))
    start = jnp.zeros((DM, HEADS, E), jnp.float32)
    grad_weight, stacked = lax.scan(step, start, (queries, keys, values, grad_out))
    return (stacked[0], stacked[1], stacked[2], grad_weight)
```

```python
import jax
import jax.numpy as jnp
from jax import lax
from jax.experimental import pallas as pl
from jax.experimental.pallas import tpu as pltpu
from jax.sharding import PartitionSpec as P

FRAMES, TOK, HEADS, E, DM = 16, 16, 16, 128, 2048
PATCH = 256
ROWS = FRAMES * HEADS
AXES = ("dp", "tm")
SCALE = 1.0 / (E**0.5)
Y, CORES_IN_PLANE = 4, 32
YROWS = DM // Y


def y_shift(n):
    total = Y * CORES_IN_PLANE
    return [(i, (i + n * CORES_IN_PLANE) % total) for i in range(total)]


def planes():
    return [[y * CORES_IN_PLANE + i for i in range(CORES_IN_PLANE)] for y in range(Y)]


def dot_nt(a, b):
    return lax.dot_general(a, b, (((1,), (1,)), ((), ())), preferred_element_type=jnp.float32)


def dot_tn(a, b):
    return lax.dot_general(a, b, (((0,), (0,)), ((), ())), preferred_element_type=jnp.float32)


def dot_nn(a, b):
    return lax.dot_general(a, b, (((1,), (0,)), ((), ())), preferred_element_type=jnp.float32)


def attend_kernel(q_ref, k_ref, v_ref, g_ref, a_ref, grads_ref):
    q = q_ref[...].reshape(ROWS, E)
    k = k_ref[...].reshape(ROWS, E)
    v = v_ref[...].reshape(ROWS, E)
    g = g_ref[...].reshape(ROWS, E)
    row = lax.broadcasted_iota(jnp.int32, (ROWS, ROWS), 0)
    col = lax.broadcasted_iota(jnp.int32, (ROWS, ROWS), 1)
    keep = (row % HEADS == col % HEADS) & (col <= row)
    scores = jnp.where(keep, dot_nt(q, k) * SCALE, -jnp.inf)
    top = jnp.max(scores, axis=1, keepdims=True)
    expd = jnp.exp(scores - top)
    probs = expd / jnp.sum(expd, axis=1, keepdims=True)
    weights = probs.astype(jnp.bfloat16)
    a_ref[...] = dot_nn(weights, v).astype(jnp.bfloat16).reshape(a_ref.shape)
    gv = dot_tn(weights, g).astype(jnp.bfloat16)
    gp = dot_nt(g, v)
    pg = probs * gp
    delta = jnp.sum(pg, axis=1, keepdims=True)
    gs = (probs * (gp - delta)).astype(jnp.bfloat16)
    gq = (dot_nn(gs, k) * SCALE).astype(jnp.bfloat16)
    gk = (dot_tn(gs, q) * SCALE).astype(jnp.bfloat16)
    block = (FRAMES, 1, 1, HEADS, E)
    grads_ref[:, 0:1] = gq.reshape(block)
    grads_ref[:, 1:2] = gk.reshape(block)
    grads_ref[:, 2:3] = gv.reshape(block)


def attend(packed, grad_attended):
    def part(n):
        return pl.BlockSpec((FRAMES, 1, 1, HEADS, E), lambda t, n=n: (0, n, t, 0, 0))

    token = pl.BlockSpec((FRAMES, 1, HEADS, E), lambda t: (0, t, 0, 0))
    return pl.pallas_call(
        attend_kernel,
        grid=(TOK,),
        in_specs=[part(0), part(1), part(2), token],
        out_specs=[token, pl.BlockSpec((FRAMES, 3, 1, HEADS, E), lambda t: (0, 0, t, 0, 0))],
        out_shape=[
            jax.ShapeDtypeStruct((FRAMES, TOK, HEADS, E), jnp.bfloat16),
            jax.ShapeDtypeStruct((FRAMES, 3, TOK, HEADS, E), jnp.bfloat16),
        ],
        compiler_params=pltpu.CompilerParams(vmem_limit_bytes=32 * 1024 * 1024),
    )(packed, packed, packed, grad_attended)


def weight_kernel(*refs):
    out = refs[-1]
    total = dot_tn(refs[0][...], refs[4][...])
    for n in range(1, Y):
        total = total + dot_tn(refs[n][...], refs[Y + n][...])
    out[...] = total.astype(jnp.bfloat16)


def weight_block(gs, atts):
    width = 512
    tokens = FRAMES * TOK
    return pl.pallas_call(
        weight_kernel,
        grid=(DM // width,),
        in_specs=[pl.BlockSpec((tokens, YROWS), lambda c: (0, 0))] * Y
        + [pl.BlockSpec((tokens, width), lambda c: (0, c))] * Y,
        out_specs=pl.BlockSpec((YROWS, width), lambda c: (0, c)),
        out_shape=jax.ShapeDtypeStruct((YROWS, DM), jnp.bfloat16),
        compiler_params=pltpu.CompilerParams(vmem_limit_bytes=32 * 1024 * 1024),
    )(*gs, *atts)


def shards(queries, keys, values, out_weight, grad_out):
    y = lax.axis_index("dp") // 2
    tiles = TOK * 2
    pieces = [t.reshape(FRAMES, tiles, 8, E) for t in (queries, keys, values)]
    pieces.append(
        grad_out.reshape(FRAMES, 2, 8, HEADS, E).transpose(0, 1, 3, 2, 4).reshape(FRAMES, tiles, 8, E)
    )
    packed = jnp.concatenate(pieces, axis=1)
    packed = lax.all_to_all(packed, "tm", split_axis=0, concat_axis=0, tiled=True)
    g_tok = (
        packed[:, 3 * tiles :]
        .reshape(FRAMES, 2, HEADS, 8, E)
        .transpose(0, 1, 3, 2, 4)
        .reshape(FRAMES * TOK, DM)
    )
    grad_attended = jnp.einsum(
        "td,dhe->the", g_tok, out_weight, preferred_element_type=jnp.float32
    ).astype(jnp.bfloat16)
    attended, grads = attend(
        packed.reshape(FRAMES, 4, TOK, HEADS, E), grad_attended.reshape(FRAMES, TOK, HEADS, E)
    )
    att = attended.reshape(FRAMES * TOK, DM)

    gs, atts = [], []
    for n in range(Y):
        cut = lax.dynamic_slice_in_dim(g_tok, lax.rem(y + n, Y) * YROWS, YROWS, axis=1)
        gs.append(cut if n == 0 else lax.ppermute(cut, AXES, y_shift(n)))
        atts.append(att if n == 0 else lax.ppermute(att, AXES, y_shift(n)))

    back = lax.all_to_all(grads, "tm", split_axis=0, concat_axis=0, tiled=True)
    shape = (1, 1, PATCH, HEADS, E)
    outs = [back[:, n].reshape(shape) for n in range(3)]

    block = weight_block(gs, atts)
    block = lax.all_to_all(
        block, AXES, split_axis=0, concat_axis=0, tiled=True, axis_index_groups=planes()
    )
    grad_weight = jnp.sum(
        block.reshape(CORES_IN_PLANE, DM // 128, HEADS, E).astype(jnp.float32), axis=0
    )
    return (*outs, grad_weight)


def solution(mesh):
    clip = P("dp", "tm", None, None, None)
    return jax.shard_map(
        shards,
        mesh=mesh,
        in_specs=(clip, clip, clip, P(), P("dp", "tm", None, None)),
        out_specs=(clip, clip, clip, P(AXES, None, None)),
        check_vma=False,
    )
```

```python
import jax
import jax.numpy as jnp
from jax import lax
from jax.experimental import pallas as pl
from jax.experimental.pallas import tpu as pltpu
from jax.sharding import PartitionSpec as P

FRAMES, TOK, HEADS, E, DM = 16, 16, 16, 128, 2048
PATCH = 256
TOKENS = FRAMES * TOK
GROUPS, GROUP = 2, 8
ROWS = FRAMES * GROUP
STEP_TOK = 4
AXES = ("dp", "tm")
SCALE = 1.0 / (E**0.5)
EXP2_SCALE = SCALE * 1.4426950408889634
Y, PLANE = 4, 32
YROWS = DM // Y
HALF = DM // 2
VMEM = 16 * 1024 * 1024


def y_shift(n):
    total = Y * PLANE
    return [(i, (i + n * PLANE) % total) for i in range(total)]


def core_swap():
    return [(i, i ^ 1) for i in range(Y * PLANE)]


def planes():
    return [[y * PLANE + i for i in range(PLANE)] for y in range(Y)]


def dot_nt(a, b):
    return lax.dot_general(a, b, (((1,), (1,)), ((), ())), preferred_element_type=jnp.float32)


def dot_tn(a, b):
    return lax.dot_general(a, b, (((0,), (0,)), ((), ())), preferred_element_type=jnp.float32)


def dot_nn(a, b):
    return lax.dot_general(a, b, (((1,), (0,)), ((), ())), preferred_element_type=jnp.float32)


def attend_group(q, k, v, g, bias):
    scores = dot_nt(q, k) + bias
    expd = jnp.exp2((scores - jnp.max(scores, axis=1, keepdims=True)) * EXP2_SCALE)
    probs = expd * (1.0 / jnp.sum(expd, axis=1, keepdims=True))
    weights = probs.astype(jnp.bfloat16)
    attended = dot_nn(weights, v).astype(jnp.bfloat16)
    gv = dot_tn(weights, g).astype(jnp.bfloat16)
    gp = dot_nt(g, v)
    delta = jnp.sum(probs * gp, axis=1, keepdims=True)
    gs = (probs * (gp - delta)).astype(jnp.bfloat16)
    gq = (dot_nn(gs, k) * SCALE).astype(jnp.bfloat16)
    gk = (dot_tn(gs, q) * SCALE).astype(jnp.bfloat16)
    return attended, gq, gk, gv


def attend_kernel(core_ref, q_ref, k_ref, v_ref, g_ref, a_ref, grads_ref, bias_ref):
    @pl.when(pl.program_id(0) == 0)
    def _():
        row = lax.broadcasted_iota(jnp.int32, (ROWS, ROWS), 0)
        col = lax.broadcasted_iota(jnp.int32, (ROWS, ROWS), 1)
        keep = (row % GROUP == col % GROUP) & (col <= row)
        bias_ref[...] = jnp.where(keep, 0.0, -jnp.inf)

    bias = bias_ref[...]
    for t in range(STEP_TOK):
        for h in range(GROUPS):
            q, k, v = (ref[:, 0, t, h].reshape(ROWS, E) for ref in (q_ref, k_ref, v_ref))
            g = g_ref[:, t, h].reshape(ROWS, E)
            attended, *grads = attend_group(q, k, v, g, bias)
            a_ref[lax.rem(core_ref[0] + h, GROUPS), :, t] = attended.reshape(FRAMES, GROUP, E)
            for n, grad in enumerate(grads):
                grads_ref[:, n, t, h] = grad.reshape(FRAMES, GROUP, E)


def attend(core, packed, grad_attended):
    def part(n):
        block = (FRAMES, 1, STEP_TOK, GROUPS, GROUP, E)
        return pl.BlockSpec(block, lambda t, n=n: (0, n, t, 0, 0, 0))

    token = pl.BlockSpec((FRAMES, STEP_TOK, GROUPS, GROUP, E), lambda t: (0, t, 0, 0, 0))
    halves = pl.BlockSpec((GROUPS, FRAMES, STEP_TOK, GROUP, E), lambda t: (0, 0, t, 0, 0))
    grads = pl.BlockSpec((FRAMES, 3, STEP_TOK, GROUPS, GROUP, E), lambda t: (0, 0, t, 0, 0, 0))
    return pl.pallas_call(
        attend_kernel,
        grid=(TOK // STEP_TOK,),
        in_specs=[pl.BlockSpec(memory_space=pltpu.SMEM), part(0), part(1), part(2), token],
        out_specs=[halves, grads],
        out_shape=[
            jax.ShapeDtypeStruct((GROUPS, FRAMES, TOK, GROUP, E), jnp.bfloat16),
            jax.ShapeDtypeStruct((FRAMES, 3, TOK, GROUPS, GROUP, E), jnp.bfloat16),
        ],
        scratch_shapes=[pltpu.VMEM((ROWS, ROWS), jnp.float32)],
        compiler_params=pltpu.CompilerParams(vmem_limit_bytes=VMEM),
        cost_estimate=pl.CostEstimate(flops=7 * 10**9, bytes_accessed=8 * 2**20, transcendentals=0),
    )(core.reshape(1), packed, packed, packed, grad_attended)


def partial_product(g_ref, g_swapped_ref, a_ref, a_swapped_ref):
    return dot_tn(g_ref[...], a_ref[...]) + dot_tn(g_swapped_ref[...], a_swapped_ref[...])


def far_kernel(plane_ref, g_ref, gs_ref, a_ref, as_ref, left_ref, right_ref):
    total = partial_product(g_ref, gs_ref, a_ref, as_ref).astype(jnp.bfloat16)
    left_ref[...] = total[:, : HALF // 2]
    right_ref[...] = total[:, HALF // 2 :]


def near_kernel(plane_ref, g1, gs1, g3, gs3, a_ref, as_ref, left_ref, right_ref, up_ref, down_ref):
    up = partial_product(g1, gs1, a_ref, as_ref)
    up_ref[:, : HALF // 2] = (up[:, : HALF // 2] + left_ref[...]).astype(jnp.bfloat16)
    up_ref[:, HALF // 2 :] = up[:, HALF // 2 :].astype(jnp.bfloat16)
    down = partial_product(g3, gs3, a_ref, as_ref)
    down_ref[:, : HALF // 2] = down[:, : HALF // 2].astype(jnp.bfloat16)
    down_ref[:, HALF // 2 :] = (down[:, HALF // 2 :] + right_ref[...]).astype(jnp.bfloat16)


def own_kernel(plane_ref, g_ref, gs_ref, a_ref, as_ref, up_ref, down_ref, out_ref):
    total = partial_product(g_ref, gs_ref, a_ref, as_ref)
    out_ref[...] = (total + up_ref[...] + down_ref[...]).astype(jnp.bfloat16)


def weight_step(kernel, plane, offsets, g, g_swapped, rest, widths):
    def rows(n):
        return pl.BlockSpec((TOKENS, YROWS), lambda i, p, n=n: (0, lax.rem(p[0] + n, Y)))

    def whole(shape):
        return pl.BlockSpec(shape, lambda i, p: (0, 0))

    specs = [rows(n) for n in offsets for _ in range(2)] + [whole(r.shape) for r in rest]
    return pl.pallas_call(
        kernel,
        grid_spec=pltpu.PrefetchScalarGridSpec(
            num_scalar_prefetch=1,
            grid=(1,),
            in_specs=specs,
            out_specs=[whole((YROWS, w)) for w in widths],
        ),
        out_shape=[jax.ShapeDtypeStruct((YROWS, w), jnp.bfloat16) for w in widths],
        compiler_params=pltpu.CompilerParams(vmem_limit_bytes=24 * 1024 * 1024),
        cost_estimate=pl.CostEstimate(
            flops=10**9 * len(offsets), bytes_accessed=4 * 2**20, transcendentals=0
        ),
    )(plane, *([g, g_swapped] * len(offsets)), *rest)


def shards(queries, keys, values, out_weight, grad_out):
    y = lax.axis_index("dp") // 2
    core = lax.rem(lax.axis_index("tm"), 2)
    tiles = TOK * 2
    pieces = [t.reshape(FRAMES, tiles, 8, E) for t in (queries, keys, values)]
    pieces.append(
        grad_out.reshape(FRAMES, 2, 8, HEADS, E).transpose(0, 1, 3, 2, 4).reshape(FRAMES, tiles, 8, E)
    )
    packed = jnp.concatenate(pieces, axis=1)
    packed = lax.all_to_all(packed, "tm", split_axis=0, concat_axis=0, tiled=True)
    g_tok = (
        packed[:, 3 * tiles :]
        .reshape(FRAMES, 2, HEADS, 8, E)
        .transpose(0, 1, 3, 2, 4)
        .reshape(TOKENS, DM)
    )

    grad_attended = jnp.einsum(
        "td,dhe->the", g_tok, out_weight, preferred_element_type=jnp.float32
    ).astype(jnp.bfloat16)
    attended, grads = attend(
        core,
        packed.reshape(FRAMES, 4, TOK, GROUPS, GROUP, E),
        grad_attended.reshape(FRAMES, TOK, GROUPS, GROUP, E),
    )

    back = lax.all_to_all(grads, "tm", split_axis=0, concat_axis=0, tiled=True)

    own = attended[0].reshape(TOKENS, HALF)
    g_swapped = lax.ppermute(g_tok, AXES, core_swap())
    other = attended[1].reshape(TOKENS, HALF)
    swapped = lax.ppermute(other, AXES, core_swap())

    plane = y.reshape(1)
    left, right = weight_step(
        far_kernel, plane, [2], g_tok, g_swapped, [own, swapped], [HALF // 2, HALF // 2]
    )
    left = lax.ppermute(left, AXES, y_shift(1))
    right = lax.ppermute(right, AXES, y_shift(-1))
    up, down = weight_step(
        near_kernel, plane, [1, 3], g_tok, g_swapped, [own, swapped, left, right], [HALF, HALF]
    )
    up = lax.ppermute(up, AXES, y_shift(1))
    down = lax.ppermute(down, AXES, y_shift(-1))
    (block,) = weight_step(
        own_kernel, plane, [0], g_tok, g_swapped, [own, swapped, up, down], [HALF]
    )

    block, back = lax.optimization_barrier((block, back))
    block = lax.all_to_all(
        block, AXES, split_axis=0, concat_axis=0, tiled=True, axis_index_groups=planes()
    )
    shape = (1, 1, PATCH, HEADS, E)
    outs = [back[:, n].reshape(shape) for n in range(3)]
    rows = DM // (Y * PLANE)
    total = jnp.sum(block.reshape(PLANE // 2, 2, rows, HALF).astype(jnp.float32), axis=0)
    grad_weight = total.transpose(1, 0, 2).reshape(rows, HEADS, E)
    return (*outs, grad_weight)


def solution(mesh):
    clip = P("dp", "tm", None, None, None)
    return jax.shard_map(
        shards,
        mesh=mesh,
        in_specs=(clip, clip, clip, P(), P("dp", "tm", None, None)),
        out_specs=(clip, clip, clip, P(AXES, None, None)),
        check_vma=False,
    )
```

```python
import jax
import jax.numpy as jnp
from jax import lax
from jax.experimental import pallas as pl
from jax.experimental.pallas import tpu as pltpu
from jax.sharding import PartitionSpec as P

FRAMES, TOK, HEADS, E, DM = 16, 16, 16, 128, 2048
PATCH = 256
TOKENS = FRAMES * TOK
GROUPS, GROUP = 2, 8
ROWS = FRAMES * GROUP
STEP_TOK = 4
AXES = ("dp", "tm")
SCALE = 1.0 / (E**0.5)
EXP2_SCALE = SCALE * 1.4426950408889634
Y, PLANE = 4, 32
YROWS = DM // Y
HALF = DM // 2
VMEM = 16 * 1024 * 1024


def y_shift(n):
    total = Y * PLANE
    return [(i, (i + n * PLANE) % total) for i in range(total)]


def core_swap():
    return [(i, i ^ 1) for i in range(Y * PLANE)]


def planes():
    return [[y * PLANE + i for i in range(PLANE)] for y in range(Y)]


def dot_nt(a, b):
    return lax.dot_general(a, b, (((1,), (1,)), ((), ())), preferred_element_type=jnp.float32)


def dot_tn(a, b):
    return lax.dot_general(a, b, (((0,), (0,)), ((), ())), preferred_element_type=jnp.float32)


def dot_nn(a, b):
    return lax.dot_general(a, b, (((1,), (0,)), ((), ())), preferred_element_type=jnp.float32)


def attend_groups(units, bias):
    scores = [dot_nt(q, k) + bias for q, k, v, g in units]
    grad_probs = [dot_nt(g, v) for q, k, v, g in units]
    expd = [jnp.exp2((s - jnp.max(s, axis=1, keepdims=True)) * EXP2_SCALE) for s in scores]
    probs = [e * (1.0 / jnp.sum(e, axis=1, keepdims=True)) for e in expd]
    weights = [p.astype(jnp.bfloat16) for p in probs]
    grad_scores = [
        (p * (gp - jnp.sum(p * gp, axis=1, keepdims=True))).astype(jnp.bfloat16)
        for p, gp in zip(probs, grad_probs)
    ]
    attended = [dot_nn(w, u[2]).astype(jnp.bfloat16) for w, u in zip(weights, units)]
    gv = [dot_tn(w, u[3]).astype(jnp.bfloat16) for w, u in zip(weights, units)]
    gq = [(dot_nn(gs, u[1]) * SCALE).astype(jnp.bfloat16) for gs, u in zip(grad_scores, units)]
    gk = [(dot_tn(gs, u[0]) * SCALE).astype(jnp.bfloat16) for gs, u in zip(grad_scores, units)]
    return attended, zip(gq, gk, gv)


def attend_kernel(q_ref, k_ref, v_ref, g_ref, own_ref, other_ref, grads_ref, bias_ref):
    @pl.when(pl.program_id(0) == 0)
    def _():
        row = lax.broadcasted_iota(jnp.int32, (ROWS, ROWS), 0)
        col = lax.broadcasted_iota(jnp.int32, (ROWS, ROWS), 1)
        keep = (row % GROUP == col % GROUP) & (col <= row)
        bias_ref[...] = jnp.where(keep, 0.0, -jnp.inf)

    bias = bias_ref[...]
    first = lax.rem(lax.axis_index("tm"), 2) == 0
    ids = [(t, h) for t in range(STEP_TOK) for h in range(GROUPS)]
    units = []
    for t, h in ids:
        parts = [ref[:, 0, t, h] for ref in (q_ref, k_ref, v_ref)] + [g_ref[:, t, h]]
        units.append([part.reshape(ROWS, E) for part in parts])
    attended, grads = attend_groups(units, bias)
    for (t, h), three in zip(ids, grads):
        for n, grad in enumerate(three):
            grads_ref[:, n, t, h] = grad.reshape(FRAMES, GROUP, E)
    for t in range(STEP_TOK):
        low, high = (a.reshape(FRAMES, GROUP, E) for a in attended[GROUPS * t : GROUPS * (t + 1)])
        own_ref[:, t] = jnp.where(first, low, high)
        other_ref[:, t] = jnp.where(first, high, low)


def attend(packed, grad_attended):
    def part(n):
        block = (FRAMES, 1, STEP_TOK, GROUPS, GROUP, E)
        return pl.BlockSpec(block, lambda t, n=n: (0, n, t, 0, 0, 0))

    token = pl.BlockSpec((FRAMES, STEP_TOK, GROUPS, GROUP, E), lambda t: (0, t, 0, 0, 0))
    half = pl.BlockSpec((FRAMES, STEP_TOK, GROUP, E), lambda t: (0, t, 0, 0))
    grads = pl.BlockSpec((FRAMES, 3, STEP_TOK, GROUPS, GROUP, E), lambda t: (0, 0, t, 0, 0, 0))
    return pl.pallas_call(
        attend_kernel,
        grid=(TOK // STEP_TOK,),
        in_specs=[part(0), part(1), part(2), token],
        out_specs=[half, half, grads],
        out_shape=[
            jax.ShapeDtypeStruct((FRAMES, TOK, GROUP, E), jnp.bfloat16),
            jax.ShapeDtypeStruct((FRAMES, TOK, GROUP, E), jnp.bfloat16),
            pltpu.HBM((FRAMES, 3, TOK, GROUPS, GROUP, E), jnp.bfloat16),
        ],
        scratch_shapes=[pltpu.VMEM((ROWS, ROWS), jnp.float32)],
        compiler_params=pltpu.CompilerParams(vmem_limit_bytes=VMEM),
        cost_estimate=pl.CostEstimate(flops=7 * 10**9, bytes_accessed=8 * 2**20, transcendentals=0),
    )(packed, packed, packed, grad_attended)


QUARTER = HALF // 2


def cut(ref, part):
    return ref[:, part * QUARTER : (part + 1) * QUARTER]


def plane_rows(ref, n):
    y = lax.div(lax.axis_index("dp"), 2)
    start = pl.multiple_of(lax.rem(y + n, Y) * YROWS, YROWS)
    return ref[:, pl.ds(start, YROWS)]


def partial_sum(n, part, g_ref, gs_ref, a_ref, as_ref):
    near = dot_tn(plane_rows(g_ref, n), cut(a_ref, part))
    return near + dot_tn(plane_rows(gs_ref, n), cut(as_ref, part))


def first_kernel(*refs):
    ins, outs = refs[:4], refs[4:]
    for out, n, part in zip(outs, (2, 2, 1, 3), (0, 1, 1, 0)):
        out[...] = partial_sum(n, part, *ins).astype(jnp.bfloat16)


def second_kernel(*refs):
    ins, came, outs = refs[:4], refs[4:6], refs[6:]
    for out, n, part, add in zip(outs, (1, 3), (0, 1), came):
        out[...] = (partial_sum(n, part, *ins) + add[...]).astype(jnp.bfloat16)


def own_kernel(*refs):
    ins, came, out = refs[:4], refs[4:8], refs[8]
    for part in range(2):
        total = partial_sum(0, part, *ins) + came[part][...] + came[2 + part][...]
        out[:, part * QUARTER : (part + 1) * QUARTER] = total.astype(jnp.bfloat16)


def weight_step(kernel, args, widths):
    whole = pl.BlockSpec(memory_space=pltpu.VMEM)
    return pl.pallas_call(
        kernel,
        in_specs=[whole] * len(args),
        out_specs=[whole] * len(widths),
        out_shape=[jax.ShapeDtypeStruct((YROWS, w), jnp.bfloat16) for w in widths],
        compiler_params=pltpu.CompilerParams(vmem_limit_bytes=VMEM),
        cost_estimate=pl.CostEstimate(flops=10**9, bytes_accessed=4 * 2**20, transcendentals=0),
    )(*args)


def shards(queries, keys, values, out_weight, grad_out):
    tiles = TOK * 2
    pieces = [t.reshape(FRAMES, tiles, 8, E) for t in (queries, keys, values)]
    pieces.append(
        grad_out.reshape(FRAMES, 2, 8, HEADS, E).transpose(0, 1, 3, 2, 4).reshape(FRAMES, tiles, 8, E)
    )
    packed = jnp.concatenate(pieces, axis=1)
    packed = lax.all_to_all(packed, "tm", split_axis=0, concat_axis=0, tiled=True)
    g_tok = (
        packed[:, 3 * tiles :]
        .reshape(FRAMES, 2, HEADS, 8, E)
        .transpose(0, 1, 3, 2, 4)
        .reshape(TOKENS, DM)
    )
    grad_attended = jnp.einsum(
        "td,dhe->the", g_tok, out_weight, preferred_element_type=jnp.float32
    ).astype(jnp.bfloat16)
    own, other, grads = attend(
        packed.reshape(FRAMES, 4, TOK, GROUPS, GROUP, E),
        grad_attended.reshape(FRAMES, TOK, GROUPS, GROUP, E),
    )

    back = lax.all_to_all(grads, "tm", split_axis=0, concat_axis=0, tiled=True)

    own = own.reshape(TOKENS, HALF)
    g_swapped = lax.ppermute(g_tok, AXES, core_swap())
    swapped = lax.ppermute(other.reshape(TOKENS, HALF), AXES, core_swap())

    ins = [g_tok, g_swapped, own, swapped]
    left, right, up1, down0 = weight_step(first_kernel, ins, [QUARTER] * 4)
    left = lax.ppermute(left, AXES, y_shift(1))
    right = lax.ppermute(right, AXES, y_shift(-1))
    up1 = lax.ppermute(up1, AXES, y_shift(1))
    down0 = lax.ppermute(down0, AXES, y_shift(-1))
    up0, down1 = weight_step(second_kernel, [*ins, left, right], [QUARTER] * 2)
    up0 = lax.ppermute(up0, AXES, y_shift(1))
    down1 = lax.ppermute(down1, AXES, y_shift(-1))
    (block,) = weight_step(own_kernel, [*ins, up0, up1, down0, down1], [HALF])

    block, back = lax.optimization_barrier((block, back))
    block = lax.all_to_all(
        block, AXES, split_axis=0, concat_axis=0, tiled=True, axis_index_groups=planes()
    )
    shape = (1, 1, PATCH, HEADS, E)
    outs = [back[:, n].reshape(shape) for n in range(3)]
    rows = DM // (Y * PLANE)
    total = jnp.sum(block.reshape(PLANE // 2, 2, rows, HALF).astype(jnp.float32), axis=0)
    grad_weight = total.transpose(1, 0, 2).reshape(rows, HEADS, E)
    return (*outs, grad_weight)


def solution(mesh):
    clip = P("dp", "tm", None, None, None)
    return jax.shard_map(
        shards,
        mesh=mesh,
        in_specs=(clip, clip, clip, P(), P("dp", "tm", None, None)),
        out_specs=(clip, clip, clip, P(AXES, None, None)),
        check_vma=False,
    )
```

```python
import jax
import jax.numpy as jnp
from jax import lax
from jax.experimental import pallas as pl
from jax.experimental.pallas import tpu as pltpu
from jax.sharding import PartitionSpec as P

FRAMES, TOK, HEADS, E, DM = 16, 16, 16, 128, 2048
PATCH = 256
TOKENS = FRAMES * TOK
GROUPS, GROUP = 2, 8
ROWS = FRAMES * GROUP
STEP_TOK = 4
AXES = ("dp", "tm")
SCALE = 1.0 / (E**0.5)
EXP2_SCALE = SCALE * 1.4426950408889634
Y, PLANE = 4, 32
YROWS = DM // Y
HALF = DM // 2
VMEM = 16 * 1024 * 1024


def y_shift(n):
    total = Y * PLANE
    return [(i, (i + n * PLANE) % total) for i in range(total)]


def core_swap():
    return [(i, i ^ 1) for i in range(Y * PLANE)]


def planes():
    return [[y * PLANE + i for i in range(PLANE)] for y in range(Y)]


def dot_nt(a, b):
    return lax.dot_general(a, b, (((1,), (1,)), ((), ())), preferred_element_type=jnp.float32)


def dot_tn(a, b):
    return lax.dot_general(a, b, (((0,), (0,)), ((), ())), preferred_element_type=jnp.float32)


def dot_nn(a, b):
    return lax.dot_general(a, b, (((1,), (0,)), ((), ())), preferred_element_type=jnp.float32)


def attend_groups(units, bias):
    scores = [dot_nt(q, k) + bias for q, k, v, g in units]
    grad_probs = [dot_nt(g, v) for q, k, v, g in units]
    expd = [jnp.exp2((s - jnp.max(s, axis=1, keepdims=True)) * EXP2_SCALE) for s in scores]
    probs = [e * (1.0 / jnp.sum(e, axis=1, keepdims=True)) for e in expd]
    weights = [p.astype(jnp.bfloat16) for p in probs]
    grad_scores = [
        (p * (gp - jnp.sum(p * gp, axis=1, keepdims=True))).astype(jnp.bfloat16)
        for p, gp in zip(probs, grad_probs)
    ]
    attended = [dot_nn(w, u[2]).astype(jnp.bfloat16) for w, u in zip(weights, units)]
    gv = [dot_tn(w, u[3]).astype(jnp.bfloat16) for w, u in zip(weights, units)]
    gq = [(dot_nn(gs, u[1]) * SCALE).astype(jnp.bfloat16) for gs, u in zip(grad_scores, units)]
    gk = [(dot_tn(gs, u[0]) * SCALE).astype(jnp.bfloat16) for gs, u in zip(grad_scores, units)]
    return attended, zip(gq, gk, gv)


def attend_kernel(q_ref, k_ref, v_ref, g_ref, own_ref, other_ref, grads_ref, bias_ref):
    @pl.when(pl.program_id(0) == 0)
    def _():
        row = lax.broadcasted_iota(jnp.int32, (ROWS, ROWS), 0)
        col = lax.broadcasted_iota(jnp.int32, (ROWS, ROWS), 1)
        keep = (row % GROUP == col % GROUP) & (col <= row)
        bias_ref[...] = jnp.where(keep, 0.0, -jnp.inf)

    bias = bias_ref[...]
    first = lax.rem(lax.axis_index("tm"), 2) == 0
    ids = [(t, h) for t in range(STEP_TOK) for h in range(GROUPS)]
    units = []
    for t, h in ids:
        parts = [ref[:, 0, t, h] for ref in (q_ref, k_ref, v_ref)] + [g_ref[:, t, h]]
        units.append([part.reshape(ROWS, E) for part in parts])
    attended, grads = attend_groups(units, bias)
    for (t, h), three in zip(ids, grads):
        for n, grad in enumerate(three):
            grads_ref[:, n, t, h] = grad.reshape(FRAMES, GROUP, E)
    for t in range(STEP_TOK):
        low, high = (a.reshape(FRAMES, GROUP, E) for a in attended[GROUPS * t : GROUPS * (t + 1)])
        own_ref[:, t] = jnp.where(first, low, high)
        other_ref[:, t] = jnp.where(first, high, low)


def attend(packed, grad_attended):
    def part(n):
        block = (FRAMES, 1, STEP_TOK, GROUPS, GROUP, E)
        return pl.BlockSpec(block, lambda t, n=n: (0, n, t, 0, 0, 0))

    token = pl.BlockSpec((FRAMES, STEP_TOK, GROUPS, GROUP, E), lambda t: (0, t, 0, 0, 0))
    half = pl.BlockSpec((FRAMES, STEP_TOK, GROUP, E), lambda t: (0, t, 0, 0))
    grads = pl.BlockSpec((FRAMES, 3, STEP_TOK, GROUPS, GROUP, E), lambda t: (0, 0, t, 0, 0, 0))
    return pl.pallas_call(
        attend_kernel,
        grid=(TOK // STEP_TOK,),
        in_specs=[part(0), part(1), part(2), token],
        out_specs=[half, half, grads],
        out_shape=[
            jax.ShapeDtypeStruct((FRAMES, TOK, GROUP, E), jnp.bfloat16),
            jax.ShapeDtypeStruct((FRAMES, TOK, GROUP, E), jnp.bfloat16),
            pltpu.HBM((FRAMES, 3, TOK, GROUPS, GROUP, E), jnp.bfloat16),
        ],
        scratch_shapes=[pltpu.VMEM((ROWS, ROWS), jnp.float32)],
        compiler_params=pltpu.CompilerParams(vmem_limit_bytes=VMEM),
        cost_estimate=pl.CostEstimate(flops=7 * 10**9, bytes_accessed=8 * 2**20, transcendentals=0),
    )(packed, packed, packed, grad_attended)


QUARTER = HALF // 2


def cut(ref, part):
    return ref[:, part * QUARTER : (part + 1) * QUARTER]


def plane_rows(ref, n):
    y = lax.div(lax.axis_index("dp"), 2)
    start = pl.multiple_of(lax.rem(y + n, Y) * YROWS, YROWS)
    return ref[:, pl.ds(start, YROWS)]


def partial_sum(n, part, g_ref, gs_ref, a_ref, as_ref):
    near = dot_tn(plane_rows(g_ref, n), cut(a_ref, part))
    return near + dot_tn(plane_rows(gs_ref, n), cut(as_ref, part))


def far_kernel(*refs):
    for part, out in enumerate(refs[4:]):
        out[...] = partial_sum(2, part, *refs[:4]).astype(jnp.bfloat16)


def direct_kernel(*refs):
    for out, n, part in zip(refs[4:], (1, 3), (1, 0)):
        out[...] = partial_sum(n, part, *refs[:4]).astype(jnp.bfloat16)


def second_kernel(*refs):
    ins, came, outs = refs[:4], refs[4:6], refs[6:]
    for out, n, part, add in zip(outs, (1, 3), (0, 1), came):
        out[...] = (partial_sum(n, part, *ins) + add[...]).astype(jnp.bfloat16)


def own_kernel(*refs):
    ins, came, outs = refs[:4], refs[4:6], refs[6:]
    for part, (out, add) in enumerate(zip(outs, came)):
        out[...] = partial_sum(0, part, *ins) + add[...]


def last_kernel(own0, own1, came0, came1, out):
    out[:, :QUARTER] = (own0[...] + came0[...]).astype(jnp.bfloat16)
    out[:, QUARTER:] = (own1[...] + came1[...]).astype(jnp.bfloat16)


def weight_step(kernel, args, widths, dtype=jnp.bfloat16):
    whole = pl.BlockSpec(memory_space=pltpu.VMEM)
    return pl.pallas_call(
        kernel,
        in_specs=[whole] * len(args),
        out_specs=[whole] * len(widths),
        out_shape=[jax.ShapeDtypeStruct((YROWS, w), dtype) for w in widths],
        compiler_params=pltpu.CompilerParams(vmem_limit_bytes=VMEM),
        cost_estimate=pl.CostEstimate(flops=2 * 10**10, bytes_accessed=4 * 2**20, transcendentals=0),
    )(*args)


def shards(queries, keys, values, out_weight, grad_out):
    tiles = TOK * 2
    pieces = [t.reshape(FRAMES, tiles, 8, E) for t in (queries, keys, values)]
    pieces.append(
        grad_out.reshape(FRAMES, 2, 8, HEADS, E).transpose(0, 1, 3, 2, 4).reshape(FRAMES, tiles, 8, E)
    )
    packed = jnp.concatenate(pieces, axis=1)
    packed = lax.all_to_all(packed, "tm", split_axis=0, concat_axis=0, tiled=True)
    g_tok = (
        packed[:, 3 * tiles :]
        .reshape(FRAMES, 2, HEADS, 8, E)
        .transpose(0, 1, 3, 2, 4)
        .reshape(TOKENS, DM)
    )
    grad_attended = jnp.einsum(
        "td,dhe->the", g_tok, out_weight, preferred_element_type=jnp.float32
    ).astype(jnp.bfloat16)
    own, other, grads = attend(
        packed.reshape(FRAMES, 4, TOK, GROUPS, GROUP, E),
        grad_attended.reshape(FRAMES, TOK, GROUPS, GROUP, E),
    )

    back = lax.all_to_all(grads, "tm", split_axis=0, concat_axis=0, tiled=True)

    own = own.reshape(TOKENS, HALF)
    g_swapped = lax.ppermute(g_tok, AXES, core_swap())
    swapped = lax.ppermute(other.reshape(TOKENS, HALF), AXES, core_swap())

    ins = [g_tok, g_swapped, own, swapped]
    pair = [QUARTER] * 2
    left, right = weight_step(far_kernel, ins, pair)
    left = lax.ppermute(left, AXES, y_shift(1))
    right = lax.ppermute(right, AXES, y_shift(-1))
    up1, down0 = weight_step(direct_kernel, ins, pair)
    up1 = lax.ppermute(up1, AXES, y_shift(1))
    down0 = lax.ppermute(down0, AXES, y_shift(-1))
    up0, down1 = weight_step(second_kernel, [*ins, left, right], pair)
    up0 = lax.ppermute(up0, AXES, y_shift(1))
    down1 = lax.ppermute(down1, AXES, y_shift(-1))
    own0, own1 = weight_step(own_kernel, [*ins, down0, up1], pair, jnp.float32)
    (block,) = weight_step(last_kernel, [own0, own1, up0, down1], [HALF])

    block, back = lax.optimization_barrier((block, back))
    block = lax.all_to_all(
        block, AXES, split_axis=0, concat_axis=0, tiled=True, axis_index_groups=planes()
    )
    shape = (1, 1, PATCH, HEADS, E)
    outs = [back[:, n].reshape(shape) for n in range(3)]
    rows = DM // (Y * PLANE)
    total = jnp.sum(block.reshape(PLANE // 2, 2, rows, HALF).astype(jnp.float32), axis=0)
    grad_weight = total.transpose(1, 0, 2).reshape(rows, HEADS, E)
    return (*outs, grad_weight)


def solution(mesh):
    clip = P("dp", "tm", None, None, None)
    return jax.shard_map(
        shards,
        mesh=mesh,
        in_specs=(clip, clip, clip, P(), P("dp", "tm", None, None)),
        out_specs=(clip, clip, clip, P(AXES, None, None)),
        check_vma=False,
    )
```

```python
import jax
import jax.numpy as jnp
from jax import lax
from jax.experimental import pallas as pl
from jax.experimental.pallas import tpu as pltpu
from jax.sharding import PartitionSpec as P

FRAMES, TOK, HEADS, E, DM = 16, 16, 16, 128, 2048
PATCH = 256
TOKENS = FRAMES * TOK
GROUPS, GROUP = 2, 8
ROWS = FRAMES * GROUP
STEP_TOK = 4
STEPS = TOK // STEP_TOK
AXES = ("dp", "tm")
SCALE = 1.0 / (E**0.5)
EXP2_SCALE = SCALE * 1.4426950408889634
Y, PLANE = 4, 32
YROWS = DM // Y
HALF = DM // 2
VMEM = 16 * 1024 * 1024


def y_shift(n):
    total = Y * PLANE
    return [(i, (i + n * PLANE) % total) for i in range(total)]


def core_swap():
    return [(i, i ^ 1) for i in range(Y * PLANE)]


def planes():
    return [[y * PLANE + i for i in range(PLANE)] for y in range(Y)]


def dot_nt(a, b):
    return lax.dot_general(a, b, (((1,), (1,)), ((), ())), preferred_element_type=jnp.float32)


def dot_tn(a, b):
    return lax.dot_general(a, b, (((0,), (0,)), ((), ())), preferred_element_type=jnp.float32)


def dot_nn(a, b):
    return lax.dot_general(a, b, (((1,), (0,)), ((), ())), preferred_element_type=jnp.float32)


def attend_groups(units, bias):
    scores = [dot_nt(k, q) + bias for q, k, v, g in units]
    grad_probs = [dot_nt(v, g) for q, k, v, g in units]
    expd = [jnp.exp2((s - jnp.max(s, axis=0, keepdims=True)) * EXP2_SCALE) for s in scores]
    probs = [e * (1.0 / jnp.sum(e, axis=0, keepdims=True)) for e in expd]
    weights = [p.astype(jnp.bfloat16) for p in probs]
    grad_scores = [
        (p * (gp - jnp.sum(p * gp, axis=0, keepdims=True))).astype(jnp.bfloat16)
        for p, gp in zip(probs, grad_probs)
    ]
    gv = [dot_nn(w, u[3]).astype(jnp.bfloat16) for w, u in zip(weights, units)]
    gk = [(dot_nn(gs, u[0]) * SCALE).astype(jnp.bfloat16) for gs, u in zip(grad_scores, units)]
    attended = [dot_tn(w, u[2]).astype(jnp.bfloat16) for w, u in zip(weights, units)]
    gq = [(dot_tn(gs, u[1]) * SCALE).astype(jnp.bfloat16) for gs, u in zip(grad_scores, units)]
    return attended, zip(gq, gk, gv)


def attend_kernel(packed_ref, g_ref, own_ref, other_ref, grads_ref, bias_ref, out_ref, sems):
    row = lax.broadcasted_iota(jnp.int32, (ROWS, ROWS), 0)
    col = lax.broadcasted_iota(jnp.int32, (ROWS, ROWS), 1)
    keep = (row % GROUP == col % GROUP) & (row <= col)
    bias_ref[...] = jnp.where(keep, 0.0, -jnp.inf)
    first = lax.rem(lax.axis_index("tm"), 2) == 0
    ids = [(t, h) for t in range(STEP_TOK) for h in range(GROUPS)]

    def out_copy(step):
        slot = step % 2
        there = grads_ref.at[:, :, pl.ds(step * STEP_TOK, STEP_TOK)]
        return pltpu.make_async_copy(out_ref.at[slot], there, sems.at[slot])

    for step in range(STEPS):
        start = step * STEP_TOK
        units = []
        for t, h in ids:
            parts = [packed_ref[:, n, start + t, h] for n in range(3)] + [g_ref[:, start + t, h]]
            units.append([part.reshape(ROWS, E) for part in parts])
        attended, grads = attend_groups(units, bias_ref[...])
        if step >= 2:
            out_copy(step - 2).wait()
        for (t, h), three in zip(ids, grads):
            for n, grad in enumerate(three):
                out_ref[step % 2, :, n, t, h] = grad.reshape(FRAMES, GROUP, E)
        out_copy(step).start()
        for t in range(STEP_TOK):
            pair = attended[GROUPS * t : GROUPS * (t + 1)]
            low, high = (a.reshape(FRAMES, GROUP, E) for a in pair)
            own_ref[:, start + t] = jnp.where(first, low, high)
            other_ref[:, start + t] = jnp.where(first, high, low)
    for step in range(max(STEPS - 2, 0), STEPS):
        out_copy(step).wait()


def attend(packed, grad_attended):
    whole = pl.BlockSpec(memory_space=pltpu.VMEM)
    half = jax.ShapeDtypeStruct((FRAMES, TOK, GROUP, E), jnp.bfloat16)
    return pl.pallas_call(
        attend_kernel,
        in_specs=[whole, whole],
        out_specs=[whole, whole, pl.BlockSpec(memory_space=pltpu.HBM)],
        out_shape=[half, half, pltpu.HBM((FRAMES, 3, TOK, GROUPS, GROUP, E), jnp.bfloat16)],
        scratch_shapes=[
            pltpu.VMEM((ROWS, ROWS), jnp.float32),
            pltpu.VMEM((2, FRAMES, 3, STEP_TOK, GROUPS, GROUP, E), jnp.bfloat16),
            pltpu.SemaphoreType.DMA((2,)),
        ],
        compiler_params=pltpu.CompilerParams(vmem_limit_bytes=VMEM),
        cost_estimate=pl.CostEstimate(flops=7 * 10**9, bytes_accessed=8 * 2**20, transcendentals=0),
    )(packed, grad_attended)


QUARTER = HALF // 2


def cut(ref, part):
    return ref[:, part * QUARTER : (part + 1) * QUARTER]


def plane_rows(ref, n):
    y = lax.div(lax.axis_index("dp"), 2)
    start = pl.multiple_of(lax.rem(y + n, Y) * YROWS, YROWS)
    return ref[:, pl.ds(start, YROWS)]


def partial_sum(n, part, g_ref, gs_ref, a_ref, as_ref):
    near = dot_tn(plane_rows(g_ref, n), cut(a_ref, part))
    return near + dot_tn(plane_rows(gs_ref, n), cut(as_ref, part))


def far_kernel(*refs):
    for part, out in enumerate(refs[4:]):
        out[...] = partial_sum(2, part, *refs[:4]).astype(jnp.bfloat16)


def direct_kernel(*refs):
    for out, n, part in zip(refs[4:], (1, 3), (1, 0)):
        out[...] = partial_sum(n, part, *refs[:4]).astype(jnp.bfloat16)


def second_kernel(*refs):
    ins, came, outs = refs[:4], refs[4:6], refs[6:]
    for out, n, part, add in zip(outs, (1, 3), (0, 1), came):
        out[...] = (partial_sum(n, part, *ins) + add[...]).astype(jnp.bfloat16)


def own_kernel(*refs):
    ins, came, outs = refs[:4], refs[4:6], refs[6:]
    for part, (out, add) in enumerate(zip(outs, came)):
        out[...] = partial_sum(0, part, *ins) + add[...]


def last_kernel(own0, own1, came0, came1, out):
    out[:, :QUARTER] = (own0[...] + came0[...]).astype(jnp.bfloat16)
    out[:, QUARTER:] = (own1[...] + came1[...]).astype(jnp.bfloat16)


def weight_step(kernel, args, widths, dtype=jnp.bfloat16):
    whole = pl.BlockSpec(memory_space=pltpu.VMEM)
    return pl.pallas_call(
        kernel,
        in_specs=[whole] * len(args),
        out_specs=[whole] * len(widths),
        out_shape=[jax.ShapeDtypeStruct((YROWS, w), dtype) for w in widths],
        compiler_params=pltpu.CompilerParams(vmem_limit_bytes=VMEM),
        cost_estimate=pl.CostEstimate(flops=2 * 10**10, bytes_accessed=4 * 2**20, transcendentals=0),
    )(*args)


def sum_kernel(in_ref, out_ref):
    total = in_ref[0].astype(jnp.float32)
    for n in range(1, in_ref.shape[0]):
        total = total + in_ref[n].astype(jnp.float32)
    for h in range(HEADS):
        c, k = divmod(h, GROUP)
        out_ref[:, h, :] = total[c, :, k * E : (k + 1) * E]


def sum_blocks(block):
    rows = DM // (Y * PLANE)
    whole = pl.BlockSpec(memory_space=pltpu.VMEM)
    return pl.pallas_call(
        sum_kernel,
        in_specs=[whole],
        out_specs=whole,
        out_shape=jax.ShapeDtypeStruct((rows, HEADS, E), jnp.float32),
        compiler_params=pltpu.CompilerParams(vmem_limit_bytes=VMEM),
    )(block.reshape(PLANE // 2, 2, rows, HALF))


def shards(queries, keys, values, out_weight, grad_out):
    tiles = TOK * 2
    pieces = [t.reshape(FRAMES, tiles, 8, E) for t in (queries, keys, values)]
    pieces.append(
        grad_out.reshape(FRAMES, 2, 8, HEADS, E).transpose(0, 1, 3, 2, 4).reshape(FRAMES, tiles, 8, E)
    )
    packed = jnp.concatenate(pieces, axis=1)
    packed = lax.all_to_all(packed, "tm", split_axis=0, concat_axis=0, tiled=True)
    g_tok = (
        packed[:, 3 * tiles :]
        .reshape(FRAMES, 2, HEADS, 8, E)
        .transpose(0, 1, 3, 2, 4)
        .reshape(TOKENS, DM)
    )
    grad_attended = jnp.einsum(
        "td,dhe->the", g_tok, out_weight, preferred_element_type=jnp.float32
    ).astype(jnp.bfloat16)
    own, other, grads = attend(
        packed.reshape(FRAMES, 4, TOK, GROUPS, GROUP, E),
        grad_attended.reshape(FRAMES, TOK, GROUPS, GROUP, E),
    )

    back = lax.all_to_all(grads, "tm", split_axis=0, concat_axis=0, tiled=True)

    own = own.reshape(TOKENS, HALF)
    g_swapped = lax.ppermute(g_tok, AXES, core_swap())
    swapped = lax.ppermute(other.reshape(TOKENS, HALF), AXES, core_swap())

    ins = [g_tok, g_swapped, own, swapped]
    pair = [QUARTER] * 2
    left, right = weight_step(far_kernel, ins, pair)
    left = lax.ppermute(left, AXES, y_shift(1))
    right = lax.ppermute(right, AXES, y_shift(-1))
    up1, down0 = weight_step(direct_kernel, ins, pair)
    up1 = lax.ppermute(up1, AXES, y_shift(1))
    down0 = lax.ppermute(down0, AXES, y_shift(-1))
    up0, down1 = weight_step(second_kernel, [*ins, left, right], pair)
    up0 = lax.ppermute(up0, AXES, y_shift(1))
    down1 = lax.ppermute(down1, AXES, y_shift(-1))
    own0, own1 = weight_step(own_kernel, [*ins, down0, up1], pair, jnp.float32)
    (block,) = weight_step(last_kernel, [own0, own1, up0, down1], [HALF])

    block, back = lax.optimization_barrier((block, back))
    block = lax.all_to_all(
        block, AXES, split_axis=0, concat_axis=0, tiled=True, axis_index_groups=planes()
    )
    shape = (1, 1, PATCH, HEADS, E)
    outs = [back[:, n].reshape(shape) for n in range(3)]
    grad_weight = sum_blocks(block)
    return (*outs, grad_weight)


def solution(mesh):
    clip = P("dp", "tm", None, None, None)
    return jax.shard_map(
        shards,
        mesh=mesh,
        in_specs=(clip, clip, clip, P(), P("dp", "tm", None, None)),
        out_specs=(clip, clip, clip, P(AXES, None, None)),
        check_vma=False,
    )
```

```python
import jax
import jax.numpy as jnp
from jax import lax
from jax.experimental import pallas as pl
from jax.experimental.pallas import tpu as pltpu
from jax.sharding import PartitionSpec as P

FRAMES, TOK, HEADS, E, DM = 16, 16, 16, 128, 2048
PATCH = 256
TOKENS = FRAMES * TOK
GROUPS, GROUP = 2, 8
ROWS = FRAMES * GROUP
STEP_TOK = 4
STEPS = TOK // STEP_TOK
AXES = ("dp", "tm")
SCALE = 1.0 / (E**0.5)
EXP2_SCALE = SCALE * 1.4426950408889634
Y, PLANE = 4, 32
YROWS = DM // Y
HALF = DM // 2
VMEM = 16 * 1024 * 1024


def y_shift(n):
    total = Y * PLANE
    return [(i, (i + n * PLANE) % total) for i in range(total)]


def core_swap():
    return [(i, i ^ 1) for i in range(Y * PLANE)]


def planes():
    return [[y * PLANE + i for i in range(PLANE)] for y in range(Y)]


def dot_nt(a, b):
    return lax.dot_general(a, b, (((1,), (1,)), ((), ())), preferred_element_type=jnp.float32)


def dot_tn(a, b):
    return lax.dot_general(a, b, (((0,), (0,)), ((), ())), preferred_element_type=jnp.float32)


def dot_nn(a, b):
    return lax.dot_general(a, b, (((1,), (0,)), ((), ())), preferred_element_type=jnp.float32)


def attend_groups(units, bias):
    scores = [dot_nt(k, q) + bias for q, k, v, g in units]
    grad_probs = [dot_nt(v, g) for q, k, v, g in units]
    expd = [jnp.exp2((s - jnp.max(s, axis=0, keepdims=True)) * EXP2_SCALE) for s in scores]
    probs = [e * (1.0 / jnp.sum(e, axis=0, keepdims=True)) for e in expd]
    weights = [p.astype(jnp.bfloat16) for p in probs]
    grad_scores = [
        (p * (gp - jnp.sum(p * gp, axis=0, keepdims=True))).astype(jnp.bfloat16)
        for p, gp in zip(probs, grad_probs)
    ]
    gv = [dot_nn(w, u[3]).astype(jnp.bfloat16) for w, u in zip(weights, units)]
    gk = [(dot_nn(gs, u[0]) * SCALE).astype(jnp.bfloat16) for gs, u in zip(grad_scores, units)]
    attended = [dot_tn(w, u[2]).astype(jnp.bfloat16) for w, u in zip(weights, units)]
    gq = [(dot_tn(gs, u[1]) * SCALE).astype(jnp.bfloat16) for gs, u in zip(grad_scores, units)]
    return attended, zip(gq, gk, gv)


def attend_kernel(packed_ref, mat_ref, own_ref, other_ref, grads_ref, bias_ref, out_ref, half_ref, g_ref, sems):
    row = lax.broadcasted_iota(jnp.int32, (ROWS, ROWS), 0)
    col = lax.broadcasted_iota(jnp.int32, (ROWS, ROWS), 1)
    keep = (row % GROUP == col % GROUP) & (row <= col)
    bias_ref[...] = jnp.where(keep, 0.0, -jnp.inf)
    mat = jnp.concatenate([mat_ref[h] for h in range(HEADS)], axis=1)
    g_ref[...] = mat.reshape(g_ref.shape)
    first = lax.rem(lax.axis_index("tm"), 2) == 0
    ids = [(t, h) for t in range(STEP_TOK) for h in range(GROUPS)]

    def out_copies(step):
        slot, tokens = step % 2, pl.ds(step * STEP_TOK, STEP_TOK)
        return (
            pltpu.make_async_copy(half_ref.at[slot], other_ref.at[:, tokens], sems.at[0, slot]),
            pltpu.make_async_copy(out_ref.at[slot], grads_ref.at[:, :, tokens], sems.at[1, slot]),
        )

    for step in range(STEPS):
        start = step * STEP_TOK
        units = []
        for t, h in ids:
            parts = [packed_ref[:, n, start + t, h] for n in range(3)] + [g_ref[:, start + t, h]]
            units.append([part.reshape(ROWS, E) for part in parts])
        attended, grads = attend_groups(units, bias_ref[...])
        if step >= 2:
            for copy in out_copies(step - 2):
                copy.wait()
        for (t, h), three in zip(ids, grads):
            for n, grad in enumerate(three):
                out_ref[step % 2, :, n, t, h] = grad.reshape(FRAMES, GROUP, E)
        for t in range(STEP_TOK):
            pair = attended[GROUPS * t : GROUPS * (t + 1)]
            low, high = (a.reshape(FRAMES, GROUP, E) for a in pair)
            own_ref[:, start + t] = jnp.where(first, low, high)
            half_ref[step % 2, :, t] = jnp.where(first, high, low)
        for copy in out_copies(step):
            copy.start()
    for step in range(max(STEPS - 2, 0), STEPS):
        for copy in out_copies(step):
            copy.wait()


def attend(packed, grad_attended):
    whole = pl.BlockSpec(memory_space=pltpu.VMEM)
    half = jax.ShapeDtypeStruct((FRAMES, TOK, GROUP, E), jnp.bfloat16)
    return pl.pallas_call(
        attend_kernel,
        in_specs=[whole, whole],
        out_specs=[whole] + [pl.BlockSpec(memory_space=pltpu.HBM)] * 2,
        out_shape=[
            half,
            pltpu.HBM(half.shape, half.dtype),
            pltpu.HBM((FRAMES, 3, TOK, GROUPS, GROUP, E), jnp.bfloat16),
        ],
        scratch_shapes=[
            pltpu.VMEM((ROWS, ROWS), jnp.float32),
            pltpu.VMEM((2, FRAMES, 3, STEP_TOK, GROUPS, GROUP, E), jnp.bfloat16),
            pltpu.VMEM((2, FRAMES, STEP_TOK, GROUP, E), jnp.bfloat16),
            pltpu.VMEM((FRAMES, TOK, GROUPS, GROUP, E), jnp.bfloat16),
            pltpu.SemaphoreType.DMA((2, 2)),
        ],
        compiler_params=pltpu.CompilerParams(vmem_limit_bytes=VMEM),
        cost_estimate=pl.CostEstimate(flops=7 * 10**9, bytes_accessed=8 * 2**20, transcendentals=0),
    )(packed, grad_attended)


QUARTER = HALF // 2


def cut(ref, part):
    return ref[:, part * QUARTER : (part + 1) * QUARTER]


def plane_rows(ref, n):
    y = lax.div(lax.axis_index("dp"), 2)
    start = pl.multiple_of(lax.rem(y + n, Y) * YROWS, YROWS)
    return ref[:, pl.ds(start, YROWS)]


def partial_sum(n, part, g_ref, gs_ref, a_ref, as_ref):
    near = dot_tn(plane_rows(g_ref, n), cut(a_ref, part))
    return near + dot_tn(plane_rows(gs_ref, n), cut(as_ref, part))


def far_kernel(*refs):
    g_ref, gs_ref, raw, raw_swapped, *outs, a_ref, as_ref = refs
    a_ref[...] = raw[...].reshape(TOKENS, HALF)
    as_ref[...] = raw_swapped[...].reshape(TOKENS, HALF)
    for part, out in enumerate(outs):
        out[...] = partial_sum(2, part, g_ref, gs_ref, a_ref, as_ref).astype(jnp.bfloat16)


def direct_kernel(*refs):
    for out, n, part in zip(refs[4:], (1, 3), (1, 0)):
        out[...] = partial_sum(n, part, *refs[:4]).astype(jnp.bfloat16)


def second_kernel(*refs):
    ins, came, outs = refs[:4], refs[4:6], refs[6:]
    for out, n, part, add in zip(outs, (1, 3), (0, 1), came):
        out[...] = (partial_sum(n, part, *ins) + add[...]).astype(jnp.bfloat16)


def own_kernel(*refs):
    ins, came, outs = refs[:4], refs[4:6], refs[6:]
    for part, (out, add) in enumerate(zip(outs, came)):
        out[...] = partial_sum(0, part, *ins) + add[...]


def last_kernel(own0, own1, came0, came1, out):
    out[:, :QUARTER] = (own0[...] + came0[...]).astype(jnp.bfloat16)
    out[:, QUARTER:] = (own1[...] + came1[...]).astype(jnp.bfloat16)


def weight_step(kernel, args, widths, dtype=jnp.bfloat16, more=()):
    whole = pl.BlockSpec(memory_space=pltpu.VMEM)
    return pl.pallas_call(
        kernel,
        in_specs=[whole] * len(args),
        out_specs=[whole] * (len(widths) + len(more)),
        out_shape=[jax.ShapeDtypeStruct((YROWS, w), dtype) for w in widths]
        + [jax.ShapeDtypeStruct(shape, jnp.bfloat16) for shape in more],
        compiler_params=pltpu.CompilerParams(vmem_limit_bytes=VMEM),
        cost_estimate=pl.CostEstimate(flops=2 * 10**10, bytes_accessed=4 * 2**20, transcendentals=0),
    )(*args)


def sum_kernel(in_ref, out_ref):
    total = in_ref[0].astype(jnp.float32)
    for n in range(1, in_ref.shape[0]):
        total = total + in_ref[n].astype(jnp.float32)
    for h in range(HEADS):
        c, k = divmod(h, GROUP)
        out_ref[:, h, :] = total[c, :, k * E : (k + 1) * E]


def sum_blocks(block):
    rows = DM // (Y * PLANE)
    whole = pl.BlockSpec(memory_space=pltpu.VMEM)
    return pl.pallas_call(
        sum_kernel,
        in_specs=[whole],
        out_specs=whole,
        out_shape=jax.ShapeDtypeStruct((rows, HEADS, E), jnp.float32),
        compiler_params=pltpu.CompilerParams(vmem_limit_bytes=VMEM),
    )(block.reshape(PLANE // 2, 2, rows, HALF))


def shards(queries, keys, values, out_weight, grad_out):
    tiles = TOK * 2
    pieces = [t.reshape(FRAMES, tiles, 8, E) for t in (queries, keys, values)]
    pieces.append(
        grad_out.reshape(FRAMES, 2, 8, HEADS, E).transpose(0, 1, 3, 2, 4).reshape(FRAMES, tiles, 8, E)
    )
    packed = jnp.concatenate(pieces, axis=1)
    packed = lax.all_to_all(packed, "tm", split_axis=0, concat_axis=0, tiled=True)
    g_tok = (
        packed[:, 3 * tiles :]
        .reshape(FRAMES, 2, HEADS, 8, E)
        .transpose(0, 1, 3, 2, 4)
        .reshape(TOKENS, DM)
    )
    grad_attended = jnp.einsum(
        "td,dhe->hte", g_tok, out_weight, preferred_element_type=jnp.float32
    ).astype(jnp.bfloat16)
    own, other, grads = attend(
        packed.reshape(FRAMES, 4, TOK, GROUPS, GROUP, E),
        grad_attended,
    )

    back = lax.all_to_all(grads, "tm", split_axis=0, concat_axis=0, tiled=True)

    own = own.reshape(TOKENS, GROUP, E)
    g_swapped = lax.ppermute(g_tok, AXES, core_swap())
    swapped = lax.ppermute(other, AXES, core_swap()).reshape(TOKENS, GROUP, E)

    ins = [g_tok, g_swapped, own, swapped]
    pair = [QUARTER] * 2
    left, right, *mats = weight_step(far_kernel, ins, pair, more=[(TOKENS, HALF)] * 2)
    ins = [g_tok, g_swapped, *mats]
    left = lax.ppermute(left, AXES, y_shift(1))
    right = lax.ppermute(right, AXES, y_shift(-1))
    up1, down0 = weight_step(direct_kernel, ins, pair)
    up1 = lax.ppermute(up1, AXES, y_shift(1))
    down0 = lax.ppermute(down0, AXES, y_shift(-1))
    up0, down1 = weight_step(second_kernel, [*ins, left, right], pair)
    up0 = lax.ppermute(up0, AXES, y_shift(1))
    down1 = lax.ppermute(down1, AXES, y_shift(-1))
    own0, own1 = weight_step(own_kernel, [*ins, down0, up1], pair, jnp.float32)
    (block,) = weight_step(last_kernel, [own0, own1, up0, down1], [HALF])

    block, back = lax.optimization_barrier((block, back))
    block = lax.all_to_all(
        block, AXES, split_axis=0, concat_axis=0, tiled=True, axis_index_groups=planes()
    )
    shape = (1, 1, PATCH, HEADS, E)
    outs = [back[:, n].reshape(shape) for n in range(3)]
    grad_weight = sum_blocks(block)
    return (*outs, grad_weight)


def solution(mesh):
    clip = P("dp", "tm", None, None, None)
    return jax.shard_map(
        shards,
        mesh=mesh,
        in_specs=(clip, clip, clip, P(), P("dp", "tm", None, None)),
        out_specs=(clip, clip, clip, P(AXES, None, None)),
        check_vma=False,
    )
```

```python
import jax
import jax.numpy as jnp
from jax import lax
from jax.experimental import pallas as pl
from jax.experimental.pallas import tpu as pltpu
from jax.sharding import PartitionSpec as P

FRAMES, TOK, HEADS, E, DM = 16, 16, 16, 128, 2048
PATCH = 256
TOKENS = FRAMES * TOK
GROUPS, GROUP = 2, 8
ROWS = FRAMES * GROUP
STEP_TOK = 8
STEPS = TOK // STEP_TOK
AXES = ("dp", "tm")
SCALE = 1.0 / (E**0.5)
EXP2_SCALE = SCALE * 1.4426950408889634
Y, PLANE = 4, 32
YROWS = DM // Y
HALF = DM // 2
VMEM = 24 * 1024 * 1024


def y_shift(n):
    total = Y * PLANE
    return [(i, (i + n * PLANE) % total) for i in range(total)]


def core_swap():
    return [(i, i ^ 1) for i in range(Y * PLANE)]


def planes():
    return [[y * PLANE + i for i in range(PLANE)] for y in range(Y)]


def dot_nt(a, b):
    return lax.dot_general(a, b, (((1,), (1,)), ((), ())), preferred_element_type=jnp.float32)


def dot_tn(a, b):
    return lax.dot_general(a, b, (((0,), (0,)), ((), ())), preferred_element_type=jnp.float32)


def dot_nn(a, b):
    return lax.dot_general(a, b, (((1,), (0,)), ((), ())), preferred_element_type=jnp.float32)


def attend_groups(units, bias):
    scores = [dot_nt(k, q) + bias for q, k, v, g in units]
    grad_probs = [dot_nt(v, g) for q, k, v, g in units]
    expd = [jnp.exp2((s - jnp.max(s, axis=0, keepdims=True)) * EXP2_SCALE) for s in scores]
    probs = [e * (1.0 / jnp.sum(e, axis=0, keepdims=True)) for e in expd]
    weights = [p.astype(jnp.bfloat16) for p in probs]
    grad_scores = [
        (p * (gp - jnp.sum(p * gp, axis=0, keepdims=True))).astype(jnp.bfloat16)
        for p, gp in zip(probs, grad_probs)
    ]
    gv = [dot_nn(w, u[3]).astype(jnp.bfloat16) for w, u in zip(weights, units)]
    gk = [(dot_nn(gs, u[0]) * SCALE).astype(jnp.bfloat16) for gs, u in zip(grad_scores, units)]
    attended = [dot_tn(w, u[2]).astype(jnp.bfloat16) for w, u in zip(weights, units)]
    gq = [(dot_tn(gs, u[1]) * SCALE).astype(jnp.bfloat16) for gs, u in zip(grad_scores, units)]
    return attended, zip(gq, gk, gv)


def attend_kernel(packed_ref, mat_ref, own_ref, other_ref, grads_ref, bias_ref, out_ref, half_ref, g_ref, sems):
    row = lax.broadcasted_iota(jnp.int32, (ROWS, ROWS), 0)
    col = lax.broadcasted_iota(jnp.int32, (ROWS, ROWS), 1)
    keep = (row % GROUP == col % GROUP) & (row <= col)
    bias_ref[...] = jnp.where(keep, 0.0, -jnp.inf)
    mat = jnp.concatenate([mat_ref[h] for h in range(HEADS)], axis=1)
    g_ref[...] = mat.reshape(g_ref.shape)
    first = lax.rem(lax.axis_index("tm"), 2) == 0
    ids = [(t, h) for t in range(STEP_TOK) for h in range(GROUPS)]

    def out_copies(step):
        slot, tokens = step % 2, pl.ds(step * STEP_TOK, STEP_TOK)
        return (
            pltpu.make_async_copy(half_ref.at[slot], other_ref.at[:, tokens], sems.at[0, slot]),
            pltpu.make_async_copy(out_ref.at[slot], grads_ref.at[:, :, tokens], sems.at[1, slot]),
        )

    for step in range(STEPS):
        start = step * STEP_TOK
        units = []
        for t, h in ids:
            parts = [packed_ref[:, n, start + t, h] for n in range(3)] + [g_ref[:, start + t, h]]
            units.append([part.reshape(ROWS, E) for part in parts])
        attended, grads = attend_groups(units, bias_ref[...])
        if step >= 2:
            for copy in out_copies(step - 2):
                copy.wait()
        for (t, h), three in zip(ids, grads):
            for n, grad in enumerate(three):
                out_ref[step % 2, :, n, t, h] = grad.reshape(FRAMES, GROUP, E)
        for t in range(STEP_TOK):
            pair = attended[GROUPS * t : GROUPS * (t + 1)]
            low, high = (a.reshape(FRAMES, GROUP, E) for a in pair)
            own_ref[:, start + t] = jnp.where(first, low, high)
            half_ref[step % 2, :, t] = jnp.where(first, high, low)
        for copy in out_copies(step):
            copy.start()
    for step in range(max(STEPS - 2, 0), STEPS):
        for copy in out_copies(step):
            copy.wait()


def attend(packed, grad_attended):
    whole = pl.BlockSpec(memory_space=pltpu.VMEM)
    half = jax.ShapeDtypeStruct((FRAMES, TOK, GROUP, E), jnp.bfloat16)
    return pl.pallas_call(
        attend_kernel,
        in_specs=[whole, whole],
        out_specs=[whole] + [pl.BlockSpec(memory_space=pltpu.HBM)] * 2,
        out_shape=[
            half,
            pltpu.HBM(half.shape, half.dtype),
            pltpu.HBM((FRAMES, 3, TOK, GROUPS, GROUP, E), jnp.bfloat16),
        ],
        scratch_shapes=[
            pltpu.VMEM((ROWS, ROWS), jnp.float32),
            pltpu.VMEM((2, FRAMES, 3, STEP_TOK, GROUPS, GROUP, E), jnp.bfloat16),
            pltpu.VMEM((2, FRAMES, STEP_TOK, GROUP, E), jnp.bfloat16),
            pltpu.VMEM((FRAMES, TOK, GROUPS, GROUP, E), jnp.bfloat16),
            pltpu.SemaphoreType.DMA((2, 2)),
        ],
        compiler_params=pltpu.CompilerParams(vmem_limit_bytes=VMEM),
        cost_estimate=pl.CostEstimate(flops=7 * 10**9, bytes_accessed=8 * 2**20, transcendentals=0),
    )(packed, grad_attended)


QUARTER = HALF // 2


def cut(ref, part):
    return ref[:, part * QUARTER : (part + 1) * QUARTER]


def plane_rows(ref, n):
    y = lax.div(lax.axis_index("dp"), 2)
    start = pl.multiple_of(lax.rem(y + n, Y) * YROWS, YROWS)
    return ref[:, pl.ds(start, YROWS)]


def partial_sum(n, part, g_ref, gs_ref, a_ref, as_ref):
    near = dot_tn(plane_rows(g_ref, n), cut(a_ref, part))
    return near + dot_tn(plane_rows(gs_ref, n), cut(as_ref, part))


def far_kernel(*refs):
    g_ref, gs_ref, raw, raw_swapped, *outs, a_ref, as_ref = refs
    a_ref[...] = raw[...].reshape(TOKENS, HALF)
    as_ref[...] = raw_swapped[...].reshape(TOKENS, HALF)
    for part, out in enumerate(outs):
        out[...] = partial_sum(2, part, g_ref, gs_ref, a_ref, as_ref).astype(jnp.bfloat16)


def direct_kernel(*refs):
    for out, n, part in zip(refs[4:], (1, 3), (1, 0)):
        out[...] = partial_sum(n, part, *refs[:4]).astype(jnp.bfloat16)


def second_kernel(*refs):
    ins, came, outs = refs[:4], refs[4:6], refs[6:]
    for out, n, part, add in zip(outs, (1, 3), (0, 1), came):
        out[...] = (partial_sum(n, part, *ins) + add[...]).astype(jnp.bfloat16)


def own_kernel(*refs):
    ins, came, outs = refs[:4], refs[4:6], refs[6:]
    for part, (out, add) in enumerate(zip(outs, came)):
        out[...] = partial_sum(0, part, *ins) + add[...]


def last_kernel(own0, own1, came0, came1, out, sum_ref, sems):
    chunk = YROWS // 4
    copies = []
    for n in range(4):
        rows = pl.ds(n * chunk, chunk)
        sum_ref[rows, :QUARTER] = (own0[rows, :] + came0[rows, :]).astype(jnp.bfloat16)
        sum_ref[rows, QUARTER:] = (own1[rows, :] + came1[rows, :]).astype(jnp.bfloat16)
        copies.append(pltpu.make_async_copy(sum_ref.at[rows], out.at[rows], sems.at[n]))
        copies[-1].start()
    for copy in copies:
        copy.wait()


def last_step(args):
    whole = pl.BlockSpec(memory_space=pltpu.VMEM)
    return pl.pallas_call(
        last_kernel,
        in_specs=[whole] * 4,
        out_specs=pl.BlockSpec(memory_space=pltpu.HBM),
        out_shape=pltpu.HBM((YROWS, HALF), jnp.bfloat16),
        scratch_shapes=[pltpu.VMEM((YROWS, HALF), jnp.bfloat16), pltpu.SemaphoreType.DMA((4,))],
        compiler_params=pltpu.CompilerParams(vmem_limit_bytes=VMEM),
        cost_estimate=pl.CostEstimate(flops=2 * 10**10, bytes_accessed=2**22, transcendentals=0),
    )(*args)


def weight_step(kernel, args, widths, dtype=jnp.bfloat16, more=()):
    whole = pl.BlockSpec(memory_space=pltpu.VMEM)
    return pl.pallas_call(
        kernel,
        in_specs=[whole] * len(args),
        out_specs=[whole] * (len(widths) + len(more)),
        out_shape=[jax.ShapeDtypeStruct((YROWS, w), dtype) for w in widths]
        + [jax.ShapeDtypeStruct(shape, jnp.bfloat16) for shape in more],
        compiler_params=pltpu.CompilerParams(vmem_limit_bytes=VMEM),
        cost_estimate=pl.CostEstimate(flops=2 * 10**10, bytes_accessed=4 * 2**20, transcendentals=0),
    )(*args)


def sum_kernel(in_ref, out_ref):
    total = in_ref[0].astype(jnp.float32)
    for n in range(1, in_ref.shape[0]):
        total = total + in_ref[n].astype(jnp.float32)
    for h in range(HEADS):
        c, k = divmod(h, GROUP)
        out_ref[:, h, :] = total[c, :, k * E : (k + 1) * E]


def sum_blocks(block):
    rows = DM // (Y * PLANE)
    whole = pl.BlockSpec(memory_space=pltpu.VMEM)
    return pl.pallas_call(
        sum_kernel,
        in_specs=[whole],
        out_specs=whole,
        out_shape=jax.ShapeDtypeStruct((rows, HEADS, E), jnp.float32),
        compiler_params=pltpu.CompilerParams(vmem_limit_bytes=VMEM),
    )(block.reshape(PLANE // 2, 2, rows, HALF))


def shards(queries, keys, values, out_weight, grad_out):
    tiles = TOK * 2
    pieces = [t.reshape(FRAMES, tiles, 8, E) for t in (queries, keys, values)]
    pieces.append(
        grad_out.reshape(FRAMES, 2, 8, HEADS, E).transpose(0, 1, 3, 2, 4).reshape(FRAMES, tiles, 8, E)
    )
    packed = jnp.concatenate(pieces, axis=1)
    packed = lax.all_to_all(packed, "tm", split_axis=0, concat_axis=0, tiled=True)
    g_tok = (
        packed[:, 3 * tiles :]
        .reshape(FRAMES, 2, HEADS, 8, E)
        .transpose(0, 1, 3, 2, 4)
        .reshape(TOKENS, DM)
    )
    grad_attended = jnp.einsum(
        "td,dhe->hte", g_tok, out_weight, preferred_element_type=jnp.float32
    ).astype(jnp.bfloat16)
    own, other, grads = attend(
        packed.reshape(FRAMES, 4, TOK, GROUPS, GROUP, E),
        grad_attended,
    )

    back = lax.all_to_all(grads, "tm", split_axis=0, concat_axis=0, tiled=True)

    own = own.reshape(TOKENS, GROUP, E)
    g_swapped = lax.ppermute(g_tok, AXES, core_swap())
    swapped = lax.ppermute(other, AXES, core_swap()).reshape(TOKENS, GROUP, E)

    ins = [g_tok, g_swapped, own, swapped]
    pair = [QUARTER] * 2
    left, right, *mats = weight_step(far_kernel, ins, pair, more=[(TOKENS, HALF)] * 2)
    ins = [g_tok, g_swapped, *mats]
    left = lax.ppermute(left, AXES, y_shift(1))
    right = lax.ppermute(right, AXES, y_shift(-1))
    up1, down0 = weight_step(direct_kernel, ins, pair)
    up1 = lax.ppermute(up1, AXES, y_shift(1))
    down0 = lax.ppermute(down0, AXES, y_shift(-1))
    up0, down1 = weight_step(second_kernel, [*ins, left, right], pair)
    up0 = lax.ppermute(up0, AXES, y_shift(1))
    down1 = lax.ppermute(down1, AXES, y_shift(-1))
    own0, own1 = weight_step(own_kernel, [*ins, down0, up1], pair, jnp.float32)
    block = last_step([own0, own1, up0, down1])

    block, back = lax.optimization_barrier((block, back))
    block = lax.all_to_all(
        block, AXES, split_axis=0, concat_axis=0, tiled=True, axis_index_groups=planes()
    )
    shape = (1, 1, PATCH, HEADS, E)
    outs = [back[:, n].reshape(shape) for n in range(3)]
    grad_weight = sum_blocks(block)
    return (*outs, grad_weight)


def solution(mesh):
    clip = P("dp", "tm", None, None, None)
    return jax.shard_map(
        shards,
        mesh=mesh,
        in_specs=(clip, clip, clip, P(), P("dp", "tm", None, None)),
        out_specs=(clip, clip, clip, P(AXES, None, None)),
        check_vma=False,
    )
```

```python
import jax
import jax.numpy as jnp
from jax import lax
from jax.experimental import pallas as pl
from jax.experimental.pallas import tpu as pltpu
from jax.sharding import PartitionSpec as P

FRAMES, TOK, HEADS, E, DM = 16, 16, 16, 128, 2048
PATCH = 256
TOKENS = FRAMES * TOK
GROUPS, GROUP = 2, 8
ROWS = FRAMES * GROUP
STEP_TOK = 8
STEPS = TOK // STEP_TOK
AXES = ("dp", "tm")
SCALE = 1.0 / (E**0.5)
EXP2_SCALE = SCALE * 1.4426950408889634
Y, PLANE = 4, 32
YROWS = DM // Y
HALF = DM // 2
VMEM = 24 * 1024 * 1024


def y_shift(n):
    total = Y * PLANE
    return [(i, (i + n * PLANE) % total) for i in range(total)]


def core_swap():
    return [(i, i ^ 1) for i in range(Y * PLANE)]


def planes():
    return [[y * PLANE + i for i in range(PLANE)] for y in range(Y)]


def dot_nt(a, b):
    return lax.dot_general(a, b, (((1,), (1,)), ((), ())), preferred_element_type=jnp.float32)


def dot_tn(a, b):
    return lax.dot_general(a, b, (((0,), (0,)), ((), ())), preferred_element_type=jnp.float32)


def dot_nn(a, b):
    return lax.dot_general(a, b, (((1,), (0,)), ((), ())), preferred_element_type=jnp.float32)


def pack_kernel(*refs):
    ins, out, sems = refs[:4], refs[4], refs[5]
    tiles = TOK * 2
    copies = [
        pltpu.make_async_copy(ref, out.at[:, pl.ds(n * tiles, tiles)], sems.at[n])
        for n, ref in enumerate(ins)
    ]
    for copy in copies:
        copy.start(priority=1)
    for copy in copies:
        copy.wait()


def pack(pieces):
    frames, tiles, rows, lanes = pieces[0].shape
    return pl.pallas_call(
        pack_kernel,
        in_specs=[pl.BlockSpec(memory_space=pltpu.HBM)] * 4,
        out_specs=pl.BlockSpec(memory_space=pltpu.VMEM),
        out_shape=jax.ShapeDtypeStruct((frames, 4 * tiles, rows, lanes), jnp.bfloat16),
        scratch_shapes=[pltpu.SemaphoreType.DMA((4,))],
        compiler_params=pltpu.CompilerParams(vmem_limit_bytes=VMEM),
    )(*(pltpu.with_memory_space_constraint(p, pltpu.HBM) for p in pieces))


def attend_groups(units, bias):
    scores = [dot_nt(k, q) + bias for q, k, v, g in units]
    grad_probs = [dot_nt(v, g) for q, k, v, g in units]
    expd = [jnp.exp2((s - jnp.max(s, axis=0, keepdims=True)) * EXP2_SCALE) for s in scores]
    probs = [e * (1.0 / jnp.sum(e, axis=0, keepdims=True)) for e in expd]
    weights = [p.astype(jnp.bfloat16) for p in probs]
    grad_scores = [
        (p * (gp - jnp.sum(p * gp, axis=0, keepdims=True))).astype(jnp.bfloat16)
        for p, gp in zip(probs, grad_probs)
    ]
    gv = [dot_nn(w, u[3]).astype(jnp.bfloat16) for w, u in zip(weights, units)]
    gk = [(dot_nn(gs, u[0]) * SCALE).astype(jnp.bfloat16) for gs, u in zip(grad_scores, units)]
    attended = [dot_tn(w, u[2]).astype(jnp.bfloat16) for w, u in zip(weights, units)]
    gq = [(dot_tn(gs, u[1]) * SCALE).astype(jnp.bfloat16) for gs, u in zip(grad_scores, units)]
    return attended, zip(gq, gk, gv)


def attend_kernel(packed_ref, mat_ref, own_ref, other_ref, grads_ref, bias_ref, out_ref, half_ref, g_ref, sems):
    row = lax.broadcasted_iota(jnp.int32, (ROWS, ROWS), 0)
    col = lax.broadcasted_iota(jnp.int32, (ROWS, ROWS), 1)
    keep = (row % GROUP == col % GROUP) & (row <= col)
    bias_ref[...] = jnp.where(keep, 0.0, -jnp.inf)
    mat = jnp.concatenate([mat_ref[h] for h in range(HEADS)], axis=1)
    g_ref[...] = mat.reshape(g_ref.shape)
    first = lax.rem(lax.axis_index("tm"), 2) == 0
    ids = [(t, h) for t in range(STEP_TOK) for h in range(GROUPS)]

    def out_copies(step):
        slot, tokens = step % 2, pl.ds(step * STEP_TOK, STEP_TOK)
        return (
            pltpu.make_async_copy(half_ref.at[slot], other_ref.at[:, tokens], sems.at[0, slot]),
            pltpu.make_async_copy(out_ref.at[slot], grads_ref.at[:, :, tokens], sems.at[1, slot]),
        )

    for step in range(STEPS):
        start = step * STEP_TOK
        units = []
        for t, h in ids:
            parts = [packed_ref[:, n, start + t, h] for n in range(3)] + [g_ref[:, start + t, h]]
            units.append([part.reshape(ROWS, E) for part in parts])
        attended, grads = attend_groups(units, bias_ref[...])
        if step >= 2:
            for copy in out_copies(step - 2):
                copy.wait()
        for (t, h), three in zip(ids, grads):
            for n, grad in enumerate(three):
                out_ref[step % 2, :, n, t, h] = grad.reshape(FRAMES, GROUP, E)
        for t in range(STEP_TOK):
            pair = attended[GROUPS * t : GROUPS * (t + 1)]
            low, high = (a.reshape(FRAMES, GROUP, E) for a in pair)
            own_ref[:, start + t] = jnp.where(first, low, high)
            half_ref[step % 2, :, t] = jnp.where(first, high, low)
        for copy in out_copies(step):
            copy.start()
    for step in range(max(STEPS - 2, 0), STEPS):
        for copy in out_copies(step):
            copy.wait()


def attend(packed, grad_attended):
    whole = pl.BlockSpec(memory_space=pltpu.VMEM)
    half = jax.ShapeDtypeStruct((FRAMES, TOK, GROUP, E), jnp.bfloat16)
    return pl.pallas_call(
        attend_kernel,
        in_specs=[whole, whole],
        out_specs=[whole] + [pl.BlockSpec(memory_space=pltpu.HBM)] * 2,
        out_shape=[
            half,
            pltpu.HBM(half.shape, half.dtype),
            pltpu.HBM((FRAMES, 3, TOK, GROUPS, GROUP, E), jnp.bfloat16),
        ],
        scratch_shapes=[
            pltpu.VMEM((ROWS, ROWS), jnp.float32),
            pltpu.VMEM((2, FRAMES, 3, STEP_TOK, GROUPS, GROUP, E), jnp.bfloat16),
            pltpu.VMEM((2, FRAMES, STEP_TOK, GROUP, E), jnp.bfloat16),
            pltpu.VMEM((FRAMES, TOK, GROUPS, GROUP, E), jnp.bfloat16),
            pltpu.SemaphoreType.DMA((2, 2)),
        ],
        compiler_params=pltpu.CompilerParams(vmem_limit_bytes=VMEM),
        cost_estimate=pl.CostEstimate(flops=7 * 10**9, bytes_accessed=8 * 2**20, transcendentals=0),
    )(packed, grad_attended)


QUARTER = HALF // 2


def cut(ref, part):
    return ref[:, part * QUARTER : (part + 1) * QUARTER]


def plane_rows(ref, n):
    y = lax.div(lax.axis_index("dp"), 2)
    start = pl.multiple_of(lax.rem(y + n, Y) * YROWS, YROWS)
    return ref[:, pl.ds(start, YROWS)]


def partial_sum(n, part, g_ref, gs_ref, a_ref, as_ref):
    near = dot_tn(plane_rows(g_ref, n), cut(a_ref, part))
    return near + dot_tn(plane_rows(gs_ref, n), cut(as_ref, part))


def far_kernel(*refs):
    g_ref, gs_ref, raw, raw_swapped, *outs, a_ref, as_ref = refs
    a_ref[...] = raw[...].reshape(TOKENS, HALF)
    as_ref[...] = raw_swapped[...].reshape(TOKENS, HALF)
    for part, out in enumerate(outs):
        out[...] = partial_sum(2, part, g_ref, gs_ref, a_ref, as_ref).astype(jnp.bfloat16)


def direct_kernel(*refs):
    for out, n, part in zip(refs[4:], (1, 3), (1, 0)):
        out[...] = partial_sum(n, part, *refs[:4]).astype(jnp.bfloat16)


def second_kernel(*refs):
    ins, came, outs = refs[:4], refs[4:6], refs[6:]
    for out, n, part, add in zip(outs, (1, 3), (0, 1), came):
        out[...] = (partial_sum(n, part, *ins) + add[...]).astype(jnp.bfloat16)


def own_kernel(*refs):
    ins, came, outs = refs[:4], refs[4:6], refs[6:]
    for part, (out, add) in enumerate(zip(outs, came)):
        out[...] = partial_sum(0, part, *ins) + add[...]


def last_kernel(own0, own1, came0, came1, out, sum_ref, sems):
    chunk = YROWS // 4
    copies = []
    for n in range(4):
        rows = pl.ds(n * chunk, chunk)
        sum_ref[rows, :QUARTER] = (own0[rows, :] + came0[rows, :]).astype(jnp.bfloat16)
        sum_ref[rows, QUARTER:] = (own1[rows, :] + came1[rows, :]).astype(jnp.bfloat16)
        copies.append(pltpu.make_async_copy(sum_ref.at[rows], out.at[rows], sems.at[n]))
        copies[-1].start()
    for copy in copies:
        copy.wait()


def last_step(args):
    whole = pl.BlockSpec(memory_space=pltpu.VMEM)
    return pl.pallas_call(
        last_kernel,
        in_specs=[whole] * 4,
        out_specs=pl.BlockSpec(memory_space=pltpu.HBM),
        out_shape=pltpu.HBM((YROWS, HALF), jnp.bfloat16),
        scratch_shapes=[pltpu.VMEM((YROWS, HALF), jnp.bfloat16), pltpu.SemaphoreType.DMA((4,))],
        compiler_params=pltpu.CompilerParams(vmem_limit_bytes=VMEM),
        cost_estimate=pl.CostEstimate(flops=2 * 10**10, bytes_accessed=2**22, transcendentals=0),
    )(*args)


def weight_step(kernel, args, widths, dtype=jnp.bfloat16, more=()):
    whole = pl.BlockSpec(memory_space=pltpu.VMEM)
    return pl.pallas_call(
        kernel,
        in_specs=[whole] * len(args),
        out_specs=[whole] * (len(widths) + len(more)),
        out_shape=[jax.ShapeDtypeStruct((YROWS, w), dtype) for w in widths]
        + [jax.ShapeDtypeStruct(shape, jnp.bfloat16) for shape in more],
        compiler_params=pltpu.CompilerParams(vmem_limit_bytes=VMEM),
        cost_estimate=pl.CostEstimate(flops=2 * 10**10, bytes_accessed=4 * 2**20, transcendentals=0),
    )(*args)


def sum_kernel(in_ref, out_ref):
    total = in_ref[0].astype(jnp.float32)
    for n in range(1, in_ref.shape[0]):
        total = total + in_ref[n].astype(jnp.float32)
    for h in range(HEADS):
        c, k = divmod(h, GROUP)
        out_ref[:, h, :] = total[c, :, k * E : (k + 1) * E]


def sum_blocks(block):
    rows = DM // (Y * PLANE)
    whole = pl.BlockSpec(memory_space=pltpu.VMEM)
    return pl.pallas_call(
        sum_kernel,
        in_specs=[whole],
        out_specs=whole,
        out_shape=jax.ShapeDtypeStruct((rows, HEADS, E), jnp.float32),
        compiler_params=pltpu.CompilerParams(vmem_limit_bytes=VMEM),
    )(block.reshape(PLANE // 2, 2, rows, HALF))


def shards(queries, keys, values, out_weight, grad_out):
    tiles = TOK * 2
    pieces = [t.reshape(FRAMES, tiles, 8, E) for t in (queries, keys, values)]
    pieces.append(
        grad_out.reshape(FRAMES, 2, 8, HEADS, E).transpose(0, 1, 3, 2, 4).reshape(FRAMES, tiles, 8, E)
    )
    packed = pack(pieces)
    packed = lax.all_to_all(packed, "tm", split_axis=0, concat_axis=0, tiled=True)
    g_tok = (
        packed[:, 3 * tiles :]
        .reshape(FRAMES, 2, HEADS, 8, E)
        .transpose(0, 1, 3, 2, 4)
        .reshape(TOKENS, DM)
    )
    grad_attended = jnp.einsum(
        "td,dhe->hte", g_tok, out_weight, preferred_element_type=jnp.float32
    ).astype(jnp.bfloat16)
    own, other, grads = attend(
        packed.reshape(FRAMES, 4, TOK, GROUPS, GROUP, E),
        grad_attended,
    )

    back = lax.all_to_all(grads, "tm", split_axis=0, concat_axis=0, tiled=True)

    own = own.reshape(TOKENS, GROUP, E)
    g_sent, other = lax.optimization_barrier((g_tok, other))
    g_swapped = lax.ppermute(g_sent, AXES, core_swap())
    swapped = lax.ppermute(other, AXES, core_swap()).reshape(TOKENS, GROUP, E)

    ins = [g_tok, g_swapped, own, swapped]
    pair = [QUARTER] * 2
    left, right, *mats = weight_step(far_kernel, ins, pair, more=[(TOKENS, HALF)] * 2)
    ins = [g_tok, g_swapped, *mats]
    left = lax.ppermute(left, AXES, y_shift(1))
    right = lax.ppermute(right, AXES, y_shift(-1))
    up1, down0 = weight_step(direct_kernel, ins, pair)
    up1 = lax.ppermute(up1, AXES, y_shift(1))
    down0 = lax.ppermute(down0, AXES, y_shift(-1))
    up0, down1 = weight_step(second_kernel, [*ins, left, right], pair)
    up0 = lax.ppermute(up0, AXES, y_shift(1))
    down1 = lax.ppermute(down1, AXES, y_shift(-1))
    own0, own1 = weight_step(own_kernel, [*ins, down0, up1], pair, jnp.float32)
    block = last_step([own0, own1, up0, down1])

    block, back = lax.optimization_barrier((block, back))
    block = lax.all_to_all(
        block, AXES, split_axis=0, concat_axis=0, tiled=True, axis_index_groups=planes()
    )
    shape = (1, 1, PATCH, HEADS, E)
    outs = [back[:, n].reshape(shape) for n in range(3)]
    grad_weight = sum_blocks(block)
    return (*outs, grad_weight)


def solution(mesh):
    clip = P("dp", "tm", None, None, None)
    return jax.shard_map(
        shards,
        mesh=mesh,
        in_specs=(clip, clip, clip, P(), P("dp", "tm", None, None)),
        out_specs=(clip, clip, clip, P(AXES, None, None)),
        check_vma=False,
    )
```

```python
import jax
import jax.numpy as jnp
from jax import lax
from jax.experimental import pallas as pl
from jax.experimental.pallas import tpu as pltpu
from jax.sharding import PartitionSpec as P

FRAMES, TOK, HEADS, E, DM = 16, 16, 16, 128, 2048
PATCH = 256
TOKENS = FRAMES * TOK
GROUPS, GROUP = 2, 8
ROWS = FRAMES * GROUP
STEP_TOK = 8
STEPS = TOK // STEP_TOK
AXES = ("dp", "tm")
SCALE = 1.0 / (E**0.5)
EXP2_SCALE = SCALE * 1.4426950408889634
Y, PLANE = 4, 32
YROWS = DM // Y
HALF = DM // 2
VMEM = 24 * 1024 * 1024


def y_shift(n):
    total = Y * PLANE
    return [(i, (i + n * PLANE) % total) for i in range(total)]


def core_swap():
    return [(i, i ^ 1) for i in range(Y * PLANE)]


def planes():
    return [[y * PLANE + i for i in range(PLANE)] for y in range(Y)]


def dot_nt(a, b):
    return lax.dot_general(a, b, (((1,), (1,)), ((), ())), preferred_element_type=jnp.float32)


def dot_tn(a, b):
    return lax.dot_general(a, b, (((0,), (0,)), ((), ())), preferred_element_type=jnp.float32)


def dot_nn(a, b):
    return lax.dot_general(a, b, (((1,), (0,)), ((), ())), preferred_element_type=jnp.float32)


def pack_kernel(*refs):
    ins, out, sems = refs[:4], refs[4], refs[5]
    tiles = TOK * 2
    copies = [
        pltpu.make_async_copy(ref, out.at[:, pl.ds(n * tiles, tiles)], sems.at[n])
        for n, ref in enumerate(ins)
    ]
    for copy in copies:
        copy.start(priority=1)
    for copy in copies:
        copy.wait()


def pack(pieces):
    frames, tiles, rows, lanes = pieces[0].shape
    return pl.pallas_call(
        pack_kernel,
        in_specs=[pl.BlockSpec(memory_space=pltpu.HBM)] * 4,
        out_specs=pl.BlockSpec(memory_space=pltpu.VMEM),
        out_shape=jax.ShapeDtypeStruct((frames, 4 * tiles, rows, lanes), jnp.bfloat16),
        scratch_shapes=[pltpu.SemaphoreType.DMA((4,))],
        compiler_params=pltpu.CompilerParams(vmem_limit_bytes=VMEM),
    )(*(pltpu.with_memory_space_constraint(p, pltpu.HBM) for p in pieces))


def attend_groups(units, bias):
    scores = [dot_nt(k, q) + bias for q, k, v, g in units]
    grad_probs = [dot_nt(v, g) for q, k, v, g in units]
    expd = [jnp.exp2((s - jnp.max(s, axis=0, keepdims=True)) * EXP2_SCALE) for s in scores]
    probs = [e * (1.0 / jnp.sum(e, axis=0, keepdims=True)) for e in expd]
    weights = [p.astype(jnp.bfloat16) for p in probs]
    grad_scores = [
        (p * (gp - jnp.sum(p * gp, axis=0, keepdims=True))).astype(jnp.bfloat16)
        for p, gp in zip(probs, grad_probs)
    ]
    yield 2, [dot_nn(w, u[3]).astype(jnp.bfloat16) for w, u in zip(weights, units)]
    yield 1, [(dot_nn(gs, u[0]) * SCALE).astype(jnp.bfloat16) for gs, u in zip(grad_scores, units)]
    yield 3, [dot_tn(w, u[2]).astype(jnp.bfloat16) for w, u in zip(weights, units)]
    yield 0, [(dot_tn(gs, u[1]) * SCALE).astype(jnp.bfloat16) for gs, u in zip(grad_scores, units)]


def attend_kernel(packed_ref, mat_ref, own_ref, other_ref, grads_ref, bias_ref, out_ref, half_ref, g_ref, sems):
    row = lax.broadcasted_iota(jnp.int32, (ROWS, ROWS), 0)
    col = lax.broadcasted_iota(jnp.int32, (ROWS, ROWS), 1)
    keep = (row % GROUP == col % GROUP) & (row <= col)
    bias_ref[...] = jnp.where(keep, 0.0, -jnp.inf)
    mat = jnp.concatenate([mat_ref[h] for h in range(HEADS)], axis=1)
    g_ref[...] = mat.reshape(g_ref.shape)
    first = lax.rem(lax.axis_index("tm"), 2) == 0
    ids = [(t, h) for t in range(STEP_TOK) for h in range(GROUPS)]

    def out_copy(step, n):
        slot, tokens = step % 2, pl.ds(step * STEP_TOK, STEP_TOK)
        if n == 3:
            here, there = half_ref.at[slot], other_ref.at[:, tokens]
        else:
            here, there = out_ref.at[slot, :, n], grads_ref.at[:, n, tokens]
        return pltpu.make_async_copy(here, there, sems.at[n, slot])

    for step in range(STEPS):
        start = step * STEP_TOK
        units = []
        for t, h in ids:
            parts = [packed_ref[:, n, start + t, h] for n in range(3)] + [g_ref[:, start + t, h]]
            units.append([part.reshape(ROWS, E) for part in parts])
        for n, values in attend_groups(units, bias_ref[...]):
            if step >= 2:
                out_copy(step - 2, n).wait()
            blocks = [value.reshape(FRAMES, GROUP, E) for value in values]
            for t in range(STEP_TOK):
                low, high = blocks[GROUPS * t : GROUPS * (t + 1)]
                if n == 3:
                    own_ref[:, start + t] = jnp.where(first, low, high)
                    half_ref[step % 2, :, t] = jnp.where(first, high, low)
                else:
                    out_ref[step % 2, :, n, t, 0] = low
                    out_ref[step % 2, :, n, t, 1] = high
            out_copy(step, n).start()
    for step in range(max(STEPS - 2, 0), STEPS):
        for n in range(4):
            out_copy(step, n).wait()


def attend(packed, grad_attended):
    whole = pl.BlockSpec(memory_space=pltpu.VMEM)
    half = jax.ShapeDtypeStruct((FRAMES, TOK, GROUP, E), jnp.bfloat16)
    return pl.pallas_call(
        attend_kernel,
        in_specs=[whole, whole],
        out_specs=[whole] + [pl.BlockSpec(memory_space=pltpu.HBM)] * 2,
        out_shape=[
            half,
            pltpu.HBM(half.shape, half.dtype),
            pltpu.HBM((FRAMES, 3, TOK, GROUPS, GROUP, E), jnp.bfloat16),
        ],
        scratch_shapes=[
            pltpu.VMEM((ROWS, ROWS), jnp.float32),
            pltpu.VMEM((2, FRAMES, 3, STEP_TOK, GROUPS, GROUP, E), jnp.bfloat16),
            pltpu.VMEM((2, FRAMES, STEP_TOK, GROUP, E), jnp.bfloat16),
            pltpu.VMEM((FRAMES, TOK, GROUPS, GROUP, E), jnp.bfloat16),
            pltpu.SemaphoreType.DMA((4, 2)),
        ],
        compiler_params=pltpu.CompilerParams(vmem_limit_bytes=VMEM),
        cost_estimate=pl.CostEstimate(flops=7 * 10**9, bytes_accessed=8 * 2**20, transcendentals=0),
    )(packed, grad_attended)


QUARTER = HALF // 2


def cut(ref, part):
    return ref[:, part * QUARTER : (part + 1) * QUARTER]


def plane_rows(ref, n):
    y = lax.div(lax.axis_index("dp"), 2)
    start = pl.multiple_of(lax.rem(y + n, Y) * YROWS, YROWS)
    return ref[:, pl.ds(start, YROWS)]


def partial_sum(n, part, g_ref, gs_ref, a_ref, as_ref):
    near = dot_tn(plane_rows(g_ref, n), cut(a_ref, part))
    return near + dot_tn(plane_rows(gs_ref, n), cut(as_ref, part))


def far_kernel(*refs):
    g_ref, gs_ref, raw, raw_swapped, *outs, a_ref, as_ref = refs
    a_ref[...] = raw[...].reshape(TOKENS, HALF)
    as_ref[...] = raw_swapped[...].reshape(TOKENS, HALF)
    for part, out in enumerate(outs):
        out[...] = partial_sum(2, part, g_ref, gs_ref, a_ref, as_ref).astype(jnp.bfloat16)


def direct_kernel(*refs):
    for out, n, part in zip(refs[4:], (1, 3), (1, 0)):
        out[...] = partial_sum(n, part, *refs[:4]).astype(jnp.bfloat16)


def second_kernel(*refs):
    ins, came, outs = refs[:4], refs[4:6], refs[6:]
    for out, n, part, add in zip(outs, (1, 3), (0, 1), came):
        out[...] = (partial_sum(n, part, *ins) + add[...]).astype(jnp.bfloat16)


def own_kernel(*refs):
    ins, came, outs = refs[:4], refs[4:6], refs[6:]
    for part, (out, add) in enumerate(zip(outs, came)):
        out[...] = partial_sum(0, part, *ins) + add[...]


def last_kernel(own0, own1, came0, came1, out, sum_ref, sems):
    chunk = YROWS // 4
    copies = []
    for n in range(4):
        rows = pl.ds(n * chunk, chunk)
        sum_ref[rows, :QUARTER] = (own0[rows, :] + came0[rows, :]).astype(jnp.bfloat16)
        sum_ref[rows, QUARTER:] = (own1[rows, :] + came1[rows, :]).astype(jnp.bfloat16)
        copies.append(pltpu.make_async_copy(sum_ref.at[rows], out.at[rows], sems.at[n]))
        copies[-1].start()
    for copy in copies:
        copy.wait()


def last_step(args):
    whole = pl.BlockSpec(memory_space=pltpu.VMEM)
    return pl.pallas_call(
        last_kernel,
        in_specs=[whole] * 4,
        out_specs=pl.BlockSpec(memory_space=pltpu.HBM),
        out_shape=pltpu.HBM((YROWS, HALF), jnp.bfloat16),
        scratch_shapes=[pltpu.VMEM((YROWS, HALF), jnp.bfloat16), pltpu.SemaphoreType.DMA((4,))],
        compiler_params=pltpu.CompilerParams(vmem_limit_bytes=VMEM),
        cost_estimate=pl.CostEstimate(flops=2 * 10**10, bytes_accessed=2**22, transcendentals=0),
    )(*args)


def weight_step(kernel, args, widths, dtype=jnp.bfloat16, more=()):
    whole = pl.BlockSpec(memory_space=pltpu.VMEM)
    return pl.pallas_call(
        kernel,
        in_specs=[whole] * len(args),
        out_specs=[whole] * (len(widths) + len(more)),
        out_shape=[jax.ShapeDtypeStruct((YROWS, w), dtype) for w in widths]
        + [jax.ShapeDtypeStruct(shape, jnp.bfloat16) for shape in more],
        compiler_params=pltpu.CompilerParams(vmem_limit_bytes=VMEM),
        cost_estimate=pl.CostEstimate(flops=2 * 10**10, bytes_accessed=4 * 2**20, transcendentals=0),
    )(*args)


def sum_kernel(in_ref, out_ref):
    total = in_ref[0].astype(jnp.float32)
    for n in range(1, in_ref.shape[0]):
        total = total + in_ref[n].astype(jnp.float32)
    for h in range(HEADS):
        c, k = divmod(h, GROUP)
        out_ref[:, h, :] = total[c, :, k * E : (k + 1) * E]


def sum_blocks(block):
    rows = DM // (Y * PLANE)
    whole = pl.BlockSpec(memory_space=pltpu.VMEM)
    return pl.pallas_call(
        sum_kernel,
        in_specs=[whole],
        out_specs=whole,
        out_shape=jax.ShapeDtypeStruct((rows, HEADS, E), jnp.float32),
        compiler_params=pltpu.CompilerParams(vmem_limit_bytes=VMEM),
    )(block.reshape(PLANE // 2, 2, rows, HALF))


def shards(queries, keys, values, out_weight, grad_out):
    tiles = TOK * 2
    pieces = [t.reshape(FRAMES, tiles, 8, E) for t in (queries, keys, values)]
    pieces.append(
        grad_out.reshape(FRAMES, 2, 8, HEADS, E).transpose(0, 1, 3, 2, 4).reshape(FRAMES, tiles, 8, E)
    )
    packed = pack(pieces)
    packed = lax.all_to_all(packed, "tm", split_axis=0, concat_axis=0, tiled=True)
    g_tok = (
        packed[:, 3 * tiles :]
        .reshape(FRAMES, 2, HEADS, 8, E)
        .transpose(0, 1, 3, 2, 4)
        .reshape(TOKENS, DM)
    )
    grad_attended = jnp.einsum(
        "td,dhe->hte", g_tok, out_weight, preferred_element_type=jnp.float32
    ).astype(jnp.bfloat16)
    own, other, grads = attend(
        packed.reshape(FRAMES, 4, TOK, GROUPS, GROUP, E),
        grad_attended,
    )

    back = lax.all_to_all(grads, "tm", split_axis=0, concat_axis=0, tiled=True)

    own = own.reshape(TOKENS, GROUP, E)
    g_sent, other = lax.optimization_barrier((g_tok, other))
    g_swapped = lax.ppermute(g_sent, AXES, core_swap())
    swapped = lax.ppermute(other, AXES, core_swap()).reshape(TOKENS, GROUP, E)

    ins = [g_tok, g_swapped, own, swapped]
    pair = [QUARTER] * 2
    left, right, *mats = weight_step(far_kernel, ins, pair, more=[(TOKENS, HALF)] * 2)
    ins = [g_tok, g_swapped, *mats]
    left = lax.ppermute(left, AXES, y_shift(1))
    right = lax.ppermute(right, AXES, y_shift(-1))
    up1, down0 = weight_step(direct_kernel, ins, pair)
    up1 = lax.ppermute(up1, AXES, y_shift(1))
    down0 = lax.ppermute(down0, AXES, y_shift(-1))
    up0, down1 = weight_step(second_kernel, [*ins, left, right], pair)
    up0 = lax.ppermute(up0, AXES, y_shift(1))
    down1 = lax.ppermute(down1, AXES, y_shift(-1))
    own0, own1 = weight_step(own_kernel, [*ins, down0, up1], pair, jnp.float32)
    block = last_step([own0, own1, up0, down1])

    block, back = lax.optimization_barrier((block, back))
    block = lax.all_to_all(
        block, AXES, split_axis=0, concat_axis=0, tiled=True, axis_index_groups=planes()
    )
    shape = (1, 1, PATCH, HEADS, E)
    outs = [back[:, n].reshape(shape) for n in range(3)]
    grad_weight = sum_blocks(block)
    return (*outs, grad_weight)


def solution(mesh):
    clip = P("dp", "tm", None, None, None)
    return jax.shard_map(
        shards,
        mesh=mesh,
        in_specs=(clip, clip, clip, P(), P("dp", "tm", None, None)),
        out_specs=(clip, clip, clip, P(AXES, None, None)),
        check_vma=False,
    )
```
